512 devices in a mesh: orb: 8 (over y, x_lo), grid: 64 (over x_hi, z, core).
Axes of the slice: x: 4 (x_hi: 2, x_lo: 2; x = x_hi * 2 + x_lo), y: 4, z: 16, core: 2. Of those that a mesh axis runs over, the one named last changes fastest.
Arguments:
- random_orbitals: float32 [8, 256, 256, 256], P('orb', 'grid'), may hold values from -6 to 6
- potential: float32 [256, 256, 256], P('grid'), may hold values from -1.5 to 0.5
- sphere_cells: int32 [1024, 2, 128], P('grid'), may hold values from 0 to 65535, as said below
- projectors: float32 [1024, 4, 128], P('grid'), may hold values from -0.9 to 0.9
- kb_energy: float32 [4], replicated, may hold values from 0.5 to 1.5
- cheb_coef: float32 [3], replicated, may hold values from 0.5 to 1.5
Outputs:
- density: float32 [256, 256, 256], P('grid')
The draws below stay inside these ranges and needn't reach their ends.
Inputs may be any that keep to these rules, and one draw needn't show every extreme that they name: `sphere_cells`: for each atom a the 128 points are distinct cells: the 128 offsets (dz, dy, dx) with |dz|, |dy|, |dx| <= 3 nearest to the atom's centre, ties broken by the order of (dz, dy, dx) from smallest to largest, added to the centre with periodic wrap along each dimension; row 0 holds the z-plane and row 1 the cell y * 256 + x. The centre's z lies in the slab of planes (a // 16) * 4 to (a // 16) * 4 + 3. Spheres of different atoms may share cells.
All inputs are finite; a program needn't handle non-finite values.
Results may differ from the reference program's by a relative error of at most 0.0002.
Values sent between devices are 32-bit elements; how exact they have to be, the bound alone decides.
A program may use at most 64 MiB of HBM per device.

```python
import math
import jax
import jax.numpy as jnp
from jax import lax

NX = 256
NY = 256
NZ = 256
SPH = 128
PROJ = 4
REACH = 3
ATOM_DEV = 16
CZ = 4
ATOMS = 1024
NSTOCH = 8


def sphere_offsets():
    width = 2 * REACH + 1
    count = width * width * width
    order_ids = jnp.arange(count, dtype=jnp.int32)
    off_z = order_ids // (width * width) - REACH
    off_y = order_ids // width % width - REACH
    off_x = order_ids % width - REACH
    radius = off_z * off_z + off_y * off_y + off_x * off_x
    ranking = jnp.argsort(radius * count + order_ids, stable=True)[:SPH]
    points = jnp.stack([off_z, off_y, off_x], axis=1)
    return points[ranking].astype(jnp.int32)


def draw_sphere_cells(key, part):
    offsets = sphere_offsets()
    key_z, key_y, key_x = jax.random.split(key, 3)
    atom_ids = jnp.arange(ATOMS)
    centre_z = atom_ids // ATOM_DEV * CZ + jax.random.randint(key_z, (ATOMS,), 0, CZ)
    centre_y = jax.random.randint(key_y, (ATOMS,), 0, NY)
    centre_x = jax.random.randint(key_x, (ATOMS,), 0, NX)
    centre_z = centre_z.at[0].set(0).at[ATOMS - 1].set(NZ - 1)
    centre_y = centre_y.at[0].set(0).at[ATOMS - 1].set(NY - 1)
    centre_x = centre_x.at[0].set(0).at[ATOMS - 1].set(NX - 1)
    cell_z = (centre_z[:, None] + offsets[None, :, 0]) % NZ
    cell_y = (centre_y[:, None] + offsets[None, :, 1]) % NY
    cell_x = (centre_x[:, None] + offsets[None, :, 2]) % NX
    in_plane = cell_y * NX + cell_x
    return jnp.stack([cell_z, in_plane], axis=1).astype(jnp.int32)


def block_levels(stream_key, dims, cuts, low, high):
    def one(axis_at, parts):
        draws = jax.random.uniform(jax.random.fold_in(jax.random.fold_in(stream_key, 6), axis_at), (parts,), jnp.float32, low / len(cuts), high / len(cuts))
        return jnp.repeat(jnp.exp(draws), dims[axis_at] // parts).reshape((-1,) + (1,) * (len(dims) - axis_at - 1))

    gain = one(*cuts[0])
    for cut in cuts[1:]:
        gain = gain * one(*cut)
    return gain


def bell_draw(key, extent, scale, most, pieces=(), kind=jnp.bfloat16):
    result = jax.random.normal(key, extent, jnp.float32) * scale
    if len(pieces) > 0:
        result = block_levels(key, extent, pieces, -0.22, 0.18) * result
    return jnp.clip(result, min=-most, max=most).astype(kind)


def setup_inputs(seed: int = 0) -> dict:
    seeds = jax.random.split(jax.random.key(seed), 7)
    return {
        "random_orbitals": bell_draw(seeds[0], (NSTOCH, NZ, NY, NX), 1.0, 6.0, ((0, 8), (1, 64)), jnp.float32),
        "potential": jnp.clip(-1.5 + 2.0 * jax.random.uniform(seeds[1], (NZ, NY, NX), jnp.float32) ** block_levels(seeds[1], (NZ, NY, NX), ((0, 64),), -0.2, 0.2), -1.5, 0.5),
        "sphere_cells": draw_sphere_cells(jax.random.fold_in(seeds[6], 71), 0),
        "projectors": bell_draw(seeds[3], (ATOMS, PROJ, SPH), 0.15, 0.9, ((0, 64),), jnp.float32),
        "kb_energy": jnp.clip(jax.random.uniform(seeds[4], (PROJ,), jnp.float32, 0.5, 1.5), 0.5, 1.5),
        "cheb_coef": jnp.clip(jax.random.uniform(seeds[5], (3,), jnp.float32, 0.5, 1.5), 0.5, 1.5),
    }


PRECISE = lax.Precision.HIGHEST
CENTRE = 2.0
HALF_RANGE = 4.0


def kinetic_table(length):
    places = jnp.arange(length)
    offset = places[:, None] - places[None, :]
    parity = jnp.where(offset % 2 == 0, 1.0, -1.0).astype(jnp.float32)
    angle_half = offset.astype(jnp.float32) * (math.pi / length)
    sine = jnp.where(offset == 0, 1.0, jnp.sin(angle_half)).astype(jnp.float32)
    off_diag = parity / (2.0 * sine * sine)
    on_diag = jnp.float32(length * length / 12.0 + 1.0 / 6.0)
    return (jnp.where(offset == 0, on_diag, off_diag) * (4.0 / (length * length))).astype(jnp.float32)


def reference(random_orbitals, potential, sphere_cells, projectors, kb_energy, cheb_coef):
    kinetic_x = kinetic_table(NX)
    kinetic_y = kinetic_table(NY)
    kinetic_z = kinetic_table(NZ)
    cell_index = (sphere_cells[:, 0, :] * (NY * NX) + sphere_cells[:, 1, :]).astype(jnp.int32)
    flat_cells = cell_index.reshape(-1)

    def apply_hamiltonian(vector):
        kinetic = jnp.dot(vector.reshape(-1, NX), kinetic_x, precision=PRECISE).reshape(vector.shape)
        kinetic = kinetic + jnp.einsum("zyx,yw->zwx", vector, kinetic_y, precision=PRECISE)
        kinetic = kinetic + jnp.einsum("zyx,zw->wyx", vector, kinetic_z, precision=PRECISE)
        values = vector.reshape(-1)[cell_index]
        coeffs = jnp.einsum("aj,apj->ap", values, projectors, precision=PRECISE) * kb_energy
        spread = jnp.einsum("ap,apj->aj", coeffs, projectors, precision=PRECISE)
        nonlocal_part = jnp.zeros((NZ * NY * NX,), jnp.float32).at[flat_cells].add(spread.reshape(-1))
        summed = kinetic + potential * vector + nonlocal_part.reshape(vector.shape)
        return (summed - CENTRE * vector) / HALF_RANGE

    def one_orbital(orb_index, density):
        orbital = random_orbitals[orb_index].astype(jnp.float32)
        first_term = apply_hamiltonian(orbital)
        second_term = 2.0 * apply_hamiltonian(first_term) - orbital
        filtered = cheb_coef[0] * orbital + cheb_coef[1] * first_term + cheb_coef[2] * second_term
        return density + filtered * filtered

    density = lax.fori_loop(0, NSTOCH, one_orbital, jnp.zeros((NZ, NY, NX), jnp.float32))
    return density / NSTOCH
```

```python
import functools

import jax
import jax.numpy as jnp
import numpy as np
from jax import lax
from jax.experimental import pallas as pl
from jax.experimental.pallas import tpu as pltpu
from jax.sharding import Mesh, PartitionSpec as P

AXES = ("y", "xl", "xh", "zb", "par", "core")
SIZES = {"y": 4, "xl": 2, "xh": 2, "zb": 8, "par": 2, "core": 2}
PLANE = ("y", "xl", "xh")
LINE = ("zb", "par", "core")
BLOCK = ("y", "xl", "xh", "par")
QUAD = ("y", "xl", "xh", "par", "core")

N = 256
REACH = 3
SPH = 128
HIGH = lax.Precision.HIGH
MESH = pl.DeviceIdType.MESH
F32 = jnp.float32


def kinetic_table(length):
    places = np.arange(length)
    offset = places[:, None] - places[None, :]
    parity = np.where(offset % 2 == 0, 1.0, -1.0)
    sine = np.where(offset == 0, 1.0, np.sin(offset * (np.pi / length)))
    table = np.where(offset == 0, length * length / 12.0 + 1.0 / 6.0, parity / (2.0 * sine * sine))
    return (table * (4.0 / (length * length))).astype(np.float32)


def sphere_offsets():
    width = 2 * REACH + 1
    count = width**3
    ids = np.arange(count)
    off = np.stack([ids // (width * width), ids // width % width, ids % width], axis=1) - REACH
    radius = (off * off).sum(axis=1)
    return off[np.argsort(radius * count + ids, kind="stable")[:SPH]]


def cube_places():
    off = sphere_offsets() + REACH
    table = np.zeros((SPH, 512), np.float32)
    table[np.arange(SPH), off[:, 1] * 64 + off[:, 0] * 8 + off[:, 2]] = 1.0
    return table


def index_of(axes):
    where = 0
    for name in axes:
        where = where * SIZES[name] + lax.axis_index(name)
    return where


def coords_of(axes, where):
    coords = {}
    for name in reversed(axes):
        coords[name] = lax.rem(where, SIZES[name])
        where = where // SIZES[name]
    return coords


def group_size(axes):
    return int(np.prod([SIZES[name] for name in axes]))


def greet_group(axes):
    me, count = index_of(axes), group_size(axes)
    barrier = pltpu.get_barrier_semaphore()

    def greet(k, carry):
        pl.semaphore_signal(
            barrier, inc=1, device_id=coords_of(axes, lax.rem(me + k, count)), device_id_type=MESH
        )
        return carry

    lax.fori_loop(1, count, greet, 0)
    return barrier, count - 1


def swap_start(axes, source, target, send, recv):
    me, count = index_of(axes), group_size(axes)

    def step(k, carry):
        peer = lax.rem(me + k, count)
        pltpu.make_async_remote_copy(
            src_ref=source(peer),
            dst_ref=target(me),
            send_sem=send.at[peer],
            recv_sem=recv.at[me],
            device_id=coords_of(axes, peer),
            device_id_type=MESH,
        ).start()
        return carry

    lax.fori_loop(1, count, step, 0)
    pltpu.make_async_copy(source(me), target(me), recv.at[me]).start()


def swap_wait(axes, source, target, send, recv):
    me, count = index_of(axes), group_size(axes)

    def step(k, carry):
        peer = lax.rem(me + k, count)
        copy = pltpu.make_async_remote_copy(
            src_ref=source(peer),
            dst_ref=target(peer),
            send_sem=send.at[peer],
            recv_sem=recv.at[peer],
            device_id=coords_of(axes, peer),
            device_id_type=MESH,
        )
        copy.wait_send()
        copy.wait_recv()
        return carry

    lax.fori_loop(1, count, step, 0)
    pltpu.make_async_copy(source(me), target(me), recv.at[me]).wait()


def comm_call(kernel, cid, outs, scratch, *operands):
    return pl.pallas_call(
        kernel,
        out_shape=[jax.ShapeDtypeStruct(shape, F32) for shape in outs],
        in_specs=[pl.BlockSpec(memory_space=pl.ANY)] * len(operands),
        out_specs=[pl.BlockSpec(memory_space=pl.ANY)] * len(outs),
        scratch_shapes=scratch,
        compiler_params=pltpu.CompilerParams(collective_id=cid, has_side_effects=True),
    )(*operands)


def dma(*shape):
    return pltpu.SemaphoreType.DMA(shape)


def spread_rows(v_ref, pot_ref, v_out, pot_out, send, recv, psend, precv):
    xh = lax.axis_index("xh")
    me = index_of(PLANE)
    barrier, greeted = greet_group(PLANE)
    pl.semaphore_wait(barrier, greeted)

    def source(peer):
        return v_ref.at[:, pl.ds(pl.multiple_of(peer * 16, 16), 16), :]

    def target(peer):
        return v_out.at[peer]

    swap_start(PLANE, source, target, send, recv)
    other = me + 1 - 2 * xh
    pot_copy = pltpu.make_async_remote_copy(
        src_ref=pot_ref.at[:, pl.ds(pl.multiple_of(other * 16, 16), 16), :],
        dst_ref=pot_out.at[xh],
        send_sem=psend.at[0],
        recv_sem=precv.at[xh],
        device_id={"xh": 1 - xh},
        device_id_type=MESH,
    )
    pot_copy.start()
    own = pltpu.make_async_copy(
        pot_ref.at[:, pl.ds(pl.multiple_of(me * 16, 16), 16), :], pot_out.at[xh], precv.at[xh]
    )
    own.start()
    swap_wait(PLANE, source, target, send, recv)
    pot_copy.wait_send()
    pltpu.make_async_remote_copy(
        src_ref=pot_ref.at[:, pl.ds(pl.multiple_of(other * 16, 16), 16), :],
        dst_ref=pot_out.at[1 - xh],
        send_sem=psend.at[0],
        recv_sem=precv.at[1 - xh],
        device_id={"xh": 1 - xh},
        device_id_type=MESH,
    ).wait_recv()
    own.wait()


def spread_planes(v_ref, pot_ref, v_out, pot_out, send, recv, psend, precv):
    barrier, greeted = greet_group(LINE)
    pl.semaphore_wait(barrier, greeted)

    def cut(peer):
        rows = pl.ds(pl.multiple_of(lax.rem(peer // 2, 2) * 8, 8), 8)
        cols = pl.ds(pl.multiple_of(lax.rem(peer, 2) * 128, 128), 128)
        return rows, cols

    def source(peer):
        rows, cols = cut(peer)
        return v_ref.at[peer // 4, :, :, rows, cols]

    def target(peer):
        return v_out.at[:, peer]

    def pot_source(peer):
        rows, cols = cut(peer)
        return pot_ref.at[:, :, rows, cols]

    def pot_target(peer):
        return pot_out.at[:, peer]

    swap_start(LINE, source, target, send, recv)
    swap_start(LINE, pot_source, pot_target, psend, precv)
    swap_wait(LINE, source, target, send, recv)
    swap_wait(LINE, pot_source, pot_target, psend, precv)


def home_of(orbital, slab):
    return {
        "y": orbital // 2,
        "xl": lax.rem(orbital, 2),
        "xh": slab // 32,
        "zb": lax.rem(slab // 4, 8),
        "par": lax.rem(slab // 2, 2),
        "core": lax.rem(slab, 2),
    }


def full(coords):
    return tuple(coords[name] for name in AXES)


def is_me(coords):
    same = coords["y"] == lax.axis_index("y")
    for name in AXES[1:]:
        same = jnp.logical_and(same, coords[name] == lax.axis_index(name))
    return same


def spread_atoms(at_ref, at_out, send, recv):
    slab = index_of(("xh", "zb", "par", "core"))
    orbital = index_of(("y", "xl"))
    odd = lax.rem(slab, 2)
    chip, near = slab // 2, lax.rem(slab // 2 + 2 * odd - 1 + 32, 32)
    barrier = pltpu.get_barrier_semaphore()
    mine, zb = index_of(BLOCK), lax.axis_index("zb")
    own = jnp.int32(0)
    homes = [home_of(zb, lax.rem(2 * mine - 1 + slot + 64, 64)) for slot in range(4)]
    sends = []
    for n, (q, slot) in enumerate(((chip, 1 + odd), (near, 3 - 3 * odd))):
        for core in range(2):
            place = coords_of(BLOCK, q)
            place["zb"] = orbital
            place["core"] = jnp.int32(core)
            sends.append((place, slot, 2 * n + core))
    for home in homes:
        same = is_me(home)
        own = own + same.astype(jnp.int32)

        @pl.when(jnp.logical_not(same))
        def _():
            pl.semaphore_signal(barrier, inc=1, device_id=full(home), device_id_type=MESH)

    pl.semaphore_wait(barrier, 4 - own)

    def each(go):
        for place, slot, n in sends:
            same = is_me(place)

            @pl.when(jnp.logical_not(same))
            def _():
                copy = pltpu.make_async_remote_copy(
                    src_ref=at_ref,
                    dst_ref=at_out.at[slot],
                    send_sem=send.at[n],
                    recv_sem=recv.at[slot],
                    device_id=full(place),
                    device_id_type=MESH,
                )
                if go:
                    copy.start()
                else:
                    copy.wait_send()

            @pl.when(same)
            def _():
                copy = pltpu.make_async_copy(at_ref, at_out.at[slot], send.at[n])
                if go:
                    copy.start()
                else:
                    copy.wait()

    each(True)
    each(False)
    for slot, home in enumerate(homes):
        @pl.when(jnp.logical_not(is_me(home)))
        def _():
            pltpu.make_async_remote_copy(
                src_ref=at_ref,
                dst_ref=at_out.at[slot],
                send_sem=send.at[0],
                recv_sem=recv.at[slot],
                device_id=full(home),
                device_id_type=MESH,
            ).wait_recv()


def to_planes(y_ref, z_out, sib_out, send, recv, ssend, srecv):
    core = lax.axis_index("core")
    barrier, greeted = greet_group(BLOCK)
    pl.semaphore_signal(barrier, inc=1, device_id={"core": 1 - core}, device_id_type=MESH)
    pl.semaphore_wait(barrier, greeted + 1)

    def source(peer):
        return y_ref.at[peer]

    def target(peer):
        return z_out.at[:, pl.ds(pl.multiple_of(peer * 8, 8), 8), :]

    swap_start(BLOCK, source, target, send, recv)
    copy = pltpu.make_async_remote_copy(
        src_ref=y_ref,
        dst_ref=sib_out,
        send_sem=ssend.at[0],
        recv_sem=srecv.at[0],
        device_id={"core": 1 - core},
        device_id_type=MESH,
    )
    copy.start()
    swap_wait(BLOCK, source, target, send, recv)
    copy.wait()


def to_rows(z_ref, y_out, send, recv):
    barrier, greeted = greet_group(BLOCK)
    pl.semaphore_wait(barrier, greeted)

    def source(peer):
        return z_ref.at[:, pl.ds(pl.multiple_of(peer * 8, 8), 8), :]

    def target(peer):
        return y_out.at[peer]

    swap_start(BLOCK, source, target, send, recv)
    swap_wait(BLOCK, source, target, send, recv)


def share_coeffs(c_ref, c_out, send, recv):
    core, me = lax.axis_index("core"), index_of(BLOCK)
    up, down = lax.rem(me + 1, 32), lax.rem(me + 31, 32)

    def place(chip, which):
        coords = coords_of(BLOCK, chip)
        coords["core"] = which
        return coords

    peers = [(place(me, 1 - core), jnp.int32(0), 0)]
    for n in range(2):
        which = lax.rem(core + n, 2)
        peers.append((place(up, which), 1 + core, 1 + which))
        peers.append((place(down, which), 3 + core, 3 + which))
    barrier = pltpu.get_barrier_semaphore()
    for coords, _, _ in peers:
        pl.semaphore_signal(barrier, inc=1, device_id=coords, device_id_type=MESH)
    pl.semaphore_wait(barrier, 5)
    copies = []
    for n, (coords, slot, _) in enumerate(peers):
        copies.append(
            pltpu.make_async_remote_copy(
                src_ref=c_ref,
                dst_ref=c_out.at[slot],
                send_sem=send.at[n],
                recv_sem=recv.at[slot],
                device_id=coords,
                device_id_type=MESH,
            )
        )
        copies[-1].start()
    for copy in copies:
        copy.wait_send()
    for slot in range(5):
        pltpu.make_async_remote_copy(
            src_ref=c_ref,
            dst_ref=c_out.at[slot],
            send_sem=send.at[0],
            recv_sem=recv.at[slot],
            device_id=peers[0][0],
            device_id_type=MESH,
        ).wait_recv()


def gather_squares(f_ref, parts_out, send, recv):
    axes = ("zb",)
    barrier, greeted = greet_group(axes)
    pl.semaphore_wait(barrier, greeted)

    def source(peer):
        return f_ref.at[:, peer]

    def target(peer):
        return parts_out.at[peer]

    swap_start(axes, source, target, send, recv)
    swap_wait(axes, source, target, send, recv)


def place_density(s_ref, out_ref, send, recv):
    barrier, greeted = greet_group(QUAD)
    pl.semaphore_wait(barrier, greeted)

    def source(peer):
        return s_ref.at[lax.rem(peer // 4, 2), lax.rem(peer // 2, 2), lax.rem(peer, 2)]

    def target(peer):
        rows = pl.ds(pl.multiple_of(peer // 2 * 8, 8), 8)
        cols = pl.ds(pl.multiple_of(lax.rem(peer, 2) * 128, 128), 128)
        return out_ref.at[:, rows, cols]

    swap_start(QUAD, source, target, send, recv)
    swap_wait(QUAD, source, target, send, recv)


def local(random_orbitals, potential, sphere_cells, projectors, kb_energy, cheb_coef):
    table = kinetic_table(N)
    chip = index_of(BLOCK)
    core = lax.axis_index("core")

    v_rows, pot_rows = comm_call(
        spread_rows, 1, [(16, 4, 16, N), (2, 4, 16, N)], [dma(16), dma(16), dma(1), dma(2)],
        random_orbitals[0], potential,
    )
    v, pot = comm_call(
        spread_planes, 2, [(2, 32, 4, 8, 128)] * 2, [dma(32)] * 4,
        v_rows.reshape(8, 2, 4, 16, N), pot_rows,
    )
    v, pot = v.reshape(N, 8, 128), pot.reshape(N, 8, 128)

    lanes = lax.broadcasted_iota(jnp.int32, (16, 128), 1)
    centres = sphere_cells[:, :, 0].astype(F32)
    marks = jnp.where(lanes == 0, centres[:, 0:1], jnp.where(lanes == 1, centres[:, 1:2], 0.0))
    packed = jnp.concatenate([projectors.reshape(64, SPH), marks], axis=0)
    (atoms,) = comm_call(spread_atoms, 3, [(4, 80, 128)], [dma(4), dma(4)], packed)
    proj = atoms[:, :64].reshape(64, 4, SPH)
    centre_z = atoms[:, 64:, 0].reshape(64).astype(jnp.int32)
    cell = atoms[:, 64:, 1].reshape(64).astype(jnp.int32)
    centre_y, centre_x = cell // N, cell % N

    steps = jnp.arange(8, dtype=jnp.int32) - REACH
    rows_hit = jnp.arange(N)[None, None, :] == ((centre_y[:, None] + steps) % N)[:, :, None]
    pick_rows = rows_hit.astype(F32).reshape(512, N)
    planes_hit = (
        8 * chip + jnp.arange(8)[None, None, :] == ((centre_z[:, None] + steps) % N)[:, :, None]
    ).astype(F32)
    cols_hit = (
        128 * core + jnp.arange(128)[None, None, :] == ((centre_x[:, None] + steps) % N)[:, :, None]
    ).astype(F32)
    cube = jnp.dot(proj.reshape(256, SPH), cube_places(), precision=lax.Precision.HIGHEST)
    cube = cube.reshape(64, 4, 8, 8, 8)
    cube = jnp.einsum("apydx,adz->apyzx", cube, planes_hit, precision=lax.Precision.HIGHEST)
    frames = jnp.einsum("apyzx,axw->apyzw", cube, cols_hit, precision=lax.Precision.HIGHEST)

    def nonlocal_term(planes):
        picked = jnp.einsum("cy,zyx->czx", pick_rows, planes, precision=HIGH).reshape(64, 1, 8, 8, 128)
        part = jnp.sum(frames * picked, axis=(2, 3, 4))
        part = jnp.pad(part.reshape(2, 128), ((0, 6), (0, 0)))
        (others,) = comm_call(share_coeffs, 4, [(5, 8, 128)], [dma(5), dma(5)], part)
        low = part[0] + others[0, 0] + others[1, 1] + others[2, 1]
        high = part[1] + others[0, 1] + others[3, 0] + others[4, 0]
        coeffs = jnp.concatenate([low, high]).reshape(64, 4) * kb_energy
        spread = jnp.sum(coeffs[:, :, None, None, None] * frames, axis=1).reshape(512, 8, 128)
        return jnp.einsum("cy,czx->zyx", pick_rows, spread, precision=HIGH)

    def apply_shifted(rows):
        planes, sibling = comm_call(
            to_planes, 5, [(8, N, 128), (32, 8, 8, 128)], [dma(32), dma(32), dma(1), dma(1)],
            rows.reshape(32, 8, 8, 128),
        )
        in_rows = jnp.einsum("wz,zrx->wrx", table, rows, precision=HIGH)
        in_rows = in_rows + jnp.dot(rows, table[:128, :128], precision=HIGH)
        in_rows = in_rows + jnp.dot(sibling.reshape(N, 8, 128), table[128:, :128], precision=HIGH)
        in_rows = in_rows + (pot - 2.0) * rows
        in_planes = jnp.einsum("wy,zyx->zwx", table, planes, precision=HIGH) + nonlocal_term(planes)
        (back,) = comm_call(to_rows, 6, [(32, 8, 8, 128)], [dma(32), dma(32)], in_planes)
        return (back.reshape(N, 8, 128) + in_rows) / 4.0

    first = apply_shifted(v)
    second = 2.0 * apply_shifted(first) - v
    filtered = cheb_coef[0] * v + cheb_coef[1] * first + cheb_coef[2] * second
    squares = (filtered * filtered).reshape(2, 8, 16, 8, 128)
    (parts,) = comm_call(gather_squares, 7, [(8, 2, 16, 8, 128)], [dma(8), dma(8)], squares)
    summed = (jnp.sum(parts, axis=0) / 8.0).reshape(2, 2, 2, 4, 8, 128)
    (density,) = comm_call(place_density, 8, [(4, N, N)], [dma(64), dma(64)], summed)
    return density


def solution(mesh):
    apart = Mesh(mesh.devices.reshape([SIZES[name] for name in AXES]), AXES)
    orb, grid = ("y", "xl"), ("xh", "zb", "par", "core")
    in_specs = (P(orb, grid), P(grid), P(grid), P(grid), P(), P())
    return jax.shard_map(local, mesh=apart, in_specs=in_specs, out_specs=P(grid), check_vma=False)
```

```python
import functools

import jax
import jax.numpy as jnp
import numpy as np
from jax import lax
from jax.experimental import pallas as pl
from jax.experimental.pallas import tpu as pltpu
from jax.sharding import Mesh, PartitionSpec as P

AXES = ("y", "xl", "xh", "zb", "par", "core")
SIZES = {"y": 4, "xl": 2, "xh": 2, "zb": 8, "par": 2, "core": 2}
PLANE = ("y", "xl", "xh")
LINE = ("zb", "par", "core")
BLOCK = ("y", "xl", "xh", "par")
QUAD = ("y", "xl", "xh", "par", "core")

N = 256
REACH = 3
SPH = 128
MESH = pl.DeviceIdType.MESH
F32 = jnp.float32


def kinetic_table(length):
    places = np.arange(length)
    offset = places[:, None] - places[None, :]
    parity = np.where(offset % 2 == 0, 1.0, -1.0)
    sine = np.where(offset == 0, 1.0, np.sin(offset * (np.pi / length)))
    table = np.where(offset == 0, length * length / 12.0 + 1.0 / 6.0, parity / (2.0 * sine * sine))
    return (table * (4.0 / (length * length))).astype(np.float32)


def sphere_offsets():
    width = 2 * REACH + 1
    count = width**3
    ids = np.arange(count)
    off = np.stack([ids // (width * width), ids // width % width, ids % width], axis=1) - REACH
    radius = (off * off).sum(axis=1)
    return off[np.argsort(radius * count + ids, kind="stable")[:SPH]]


def index_of(axes):
    where = 0
    for name in axes:
        where = where * SIZES[name] + lax.axis_index(name)
    return where


def coords_of(axes, where):
    coords = {}
    for name in reversed(axes):
        coords[name] = lax.rem(where, SIZES[name])
        where = where // SIZES[name]
    return coords


def group_size(axes):
    return int(np.prod([SIZES[name] for name in axes]))


def greet_group(axes):
    me, count = index_of(axes), group_size(axes)
    barrier = pltpu.get_barrier_semaphore()

    def greet(k, carry):
        pl.semaphore_signal(
            barrier, inc=1, device_id=coords_of(axes, lax.rem(me + k, count)), device_id_type=MESH
        )
        return carry

    lax.fori_loop(1, count, greet, 0)
    return barrier, count - 1


def swap_start(axes, source, target, send, recv):
    me, count = index_of(axes), group_size(axes)

    def step(k, carry):
        peer = lax.rem(me + k, count)
        pltpu.make_async_remote_copy(
            src_ref=source(peer),
            dst_ref=target(me),
            send_sem=send.at[peer],
            recv_sem=recv.at[me],
            device_id=coords_of(axes, peer),
            device_id_type=MESH,
        ).start()
        return carry

    lax.fori_loop(1, count, step, 0)
    pltpu.make_async_copy(source(me), target(me), recv.at[me]).start()


def swap_wait(axes, source, target, send, recv):
    me, count = index_of(axes), group_size(axes)

    def step(k, carry):
        peer = lax.rem(me + k, count)
        copy = pltpu.make_async_remote_copy(
            src_ref=source(peer),
            dst_ref=target(peer),
            send_sem=send.at[peer],
            recv_sem=recv.at[peer],
            device_id=coords_of(axes, peer),
            device_id_type=MESH,
        )
        copy.wait_send()
        copy.wait_recv()
        return carry

    lax.fori_loop(1, count, step, 0)
    pltpu.make_async_copy(source(me), target(me), recv.at[me]).wait()


def comm_call(kernel, cid, outs, scratch, *operands):
    return pl.pallas_call(
        kernel,
        out_shape=[jax.ShapeDtypeStruct(shape, F32) for shape in outs],
        in_specs=[pl.BlockSpec(memory_space=pl.ANY)] * len(operands),
        out_specs=[pl.BlockSpec(memory_space=pl.ANY)] * len(outs),
        scratch_shapes=scratch,
        compiler_params=pltpu.CompilerParams(collective_id=cid, has_side_effects=True),
    )(*operands)


def dma(*shape):
    return pltpu.SemaphoreType.DMA(shape)


def spread_rows(v_ref, pot_ref, v_out, pot_out, send, recv, psend, precv):
    xh = lax.axis_index("xh")
    me = index_of(PLANE)
    barrier, greeted = greet_group(PLANE)
    pl.semaphore_wait(barrier, greeted)

    def source(peer):
        return v_ref.at[:, pl.ds(pl.multiple_of(peer * 16, 16), 16), :]

    def target(peer):
        return v_out.at[peer]

    swap_start(PLANE, source, target, send, recv)
    other = me + 1 - 2 * xh
    pot_copy = pltpu.make_async_remote_copy(
        src_ref=pot_ref.at[:, pl.ds(pl.multiple_of(other * 16, 16), 16), :],
        dst_ref=pot_out.at[xh],
        send_sem=psend.at[0],
        recv_sem=precv.at[xh],
        device_id={"xh": 1 - xh},
        device_id_type=MESH,
    )
    pot_copy.start()
    own = pltpu.make_async_copy(
        pot_ref.at[:, pl.ds(pl.multiple_of(me * 16, 16), 16), :], pot_out.at[xh], precv.at[xh]
    )
    own.start()
    swap_wait(PLANE, source, target, send, recv)
    pot_copy.wait_send()
    pltpu.make_async_remote_copy(
        src_ref=pot_ref.at[:, pl.ds(pl.multiple_of(other * 16, 16), 16), :],
        dst_ref=pot_out.at[1 - xh],
        send_sem=psend.at[0],
        recv_sem=precv.at[1 - xh],
        device_id={"xh": 1 - xh},
        device_id_type=MESH,
    ).wait_recv()
    own.wait()


def spread_planes(v_ref, pot_ref, v_out, pot_out, send, recv, psend, precv):
    barrier, greeted = greet_group(LINE)
    pl.semaphore_wait(barrier, greeted)

    def cut(peer):
        rows = pl.ds(pl.multiple_of(lax.rem(peer // 2, 2) * 8, 8), 8)
        cols = pl.ds(pl.multiple_of(lax.rem(peer, 2) * 128, 128), 128)
        return rows, cols

    def source(peer):
        rows, cols = cut(peer)
        return v_ref.at[peer // 4, :, :, rows, cols]

    def target(peer):
        return v_out.at[:, peer]

    def pot_source(peer):
        rows, cols = cut(peer)
        return pot_ref.at[:, :, rows, cols]

    def pot_target(peer):
        return pot_out.at[:, peer]

    swap_start(LINE, source, target, send, recv)
    swap_start(LINE, pot_source, pot_target, psend, precv)
    swap_wait(LINE, source, target, send, recv)
    swap_wait(LINE, pot_source, pot_target, psend, precv)


def home_of(orbital, slab):
    return {
        "y": orbital // 2,
        "xl": lax.rem(orbital, 2),
        "xh": slab // 32,
        "zb": lax.rem(slab // 4, 8),
        "par": lax.rem(slab // 2, 2),
        "core": lax.rem(slab, 2),
    }


def full(coords):
    return tuple(coords[name] for name in AXES)


def is_me(coords):
    same = coords["y"] == lax.axis_index("y")
    for name in AXES[1:]:
        same = jnp.logical_and(same, coords[name] == lax.axis_index(name))
    return same


def spread_atoms(at_ref, at_out, send, recv):
    slab = index_of(("xh", "zb", "par", "core"))
    orbital = index_of(("y", "xl"))
    odd = lax.rem(slab, 2)
    chip, near = slab // 2, lax.rem(slab // 2 + 2 * odd - 1 + 32, 32)
    barrier = pltpu.get_barrier_semaphore()
    mine, zb = index_of(BLOCK), lax.axis_index("zb")
    own = jnp.int32(0)
    homes = [home_of(zb, lax.rem(2 * mine - 1 + slot + 64, 64)) for slot in range(4)]
    sends = []
    for n, (q, slot) in enumerate(((chip, 1 + odd), (near, 3 - 3 * odd))):
        for core in range(2):
            place = coords_of(BLOCK, q)
            place["zb"] = orbital
            place["core"] = jnp.int32(core)
            sends.append((place, slot, 2 * n + core))
    for home in homes:
        same = is_me(home)
        own = own + same.astype(jnp.int32)

        @pl.when(jnp.logical_not(same))
        def _():
            pl.semaphore_signal(barrier, inc=1, device_id=full(home), device_id_type=MESH)

    pl.semaphore_wait(barrier, 4 - own)

    def each(go):
        for place, slot, n in sends:
            same = is_me(place)

            @pl.when(jnp.logical_not(same))
            def _():
                copy = pltpu.make_async_remote_copy(
                    src_ref=at_ref,
                    dst_ref=at_out.at[slot],
                    send_sem=send.at[n],
                    recv_sem=recv.at[slot],
                    device_id=full(place),
                    device_id_type=MESH,
                )
                if go:
                    copy.start()
                else:
                    copy.wait_send()

            @pl.when(same)
            def _():
                copy = pltpu.make_async_copy(at_ref, at_out.at[slot], send.at[n])
                if go:
                    copy.start()
                else:
                    copy.wait()

    each(True)
    each(False)
    for slot, home in enumerate(homes):
        @pl.when(jnp.logical_not(is_me(home)))
        def _():
            pltpu.make_async_remote_copy(
                src_ref=at_ref,
                dst_ref=at_out.at[slot],
                send_sem=send.at[0],
                recv_sem=recv.at[slot],
                device_id=full(home),
                device_id_type=MESH,
            ).wait_recv()


def gather_squares(f_ref, parts_out, send, recv):
    axes = ("zb",)
    barrier, greeted = greet_group(axes)
    pl.semaphore_wait(barrier, greeted)

    def source(peer):
        return f_ref.at[:, peer]

    def target(peer):
        return parts_out.at[peer]

    swap_start(axes, source, target, send, recv)
    swap_wait(axes, source, target, send, recv)


def place_density(s_ref, out_ref, send, recv):
    barrier, greeted = greet_group(QUAD)
    pl.semaphore_wait(barrier, greeted)

    def source(peer):
        return s_ref.at[lax.rem(peer // 4, 2), lax.rem(peer // 2, 2), lax.rem(peer, 2)]

    def target(peer):
        rows = pl.ds(pl.multiple_of(peer // 2 * 8, 8), 8)
        cols = pl.ds(pl.multiple_of(lax.rem(peer, 2) * 128, 128), 128)
        return out_ref.at[:, rows, cols]

    swap_start(QUAD, source, target, send, recv)
    swap_wait(QUAD, source, target, send, recv)


def split3(table):
    high = table.astype(jnp.bfloat16)
    low = (table - high.astype(np.float32)).astype(jnp.bfloat16)
    return high, low


def split(x):
    high = x.astype(jnp.bfloat16)
    return high, (x - high.astype(F32)).astype(jnp.bfloat16)


def mm(a, b):
    return lax.dot_general(a, b, (((1,), (0,)), ((), ())), preferred_element_type=F32)


def mm_nt(a, b):
    return lax.dot_general(a, b, (((1,), (1,)), ((), ())), preferred_element_type=F32)


def wrapped(x):
    x = jnp.where(x < 0.0, x + 256.0, x)
    return jnp.where(x > 255.0, x - 256.0, x)


def along_z(x_ref, out_ref, kl_ref):
    table = kl_ref[...]
    for pair in range(4):
        x = jnp.concatenate([x_ref[:, 2 * pair, :], x_ref[:, 2 * pair + 1, :]], axis=1)
        high, low = split(x)
        res = mm(table, jnp.concatenate([high, low, high], axis=0))
        out_ref[:, 2 * pair, :] = res[:, :128]
        out_ref[:, 2 * pair + 1, :] = res[:, 128:]


def along_x(x_ref, sib_ref, pot_ref, out_ref, kr_ref):
    def step(n, carry):
        zs = pl.ds(n * 32, 32)
        x = x_ref[zs]
        both = jnp.concatenate([x.reshape(256, 128), sib_ref[zs].reshape(256, 128)], axis=1)
        high, low = split(both)
        res = mm(jnp.concatenate([high, low, high], axis=1), kr_ref[...])
        out_ref[zs] += res.reshape(32, 8, 128) + (pot_ref[zs] - 2.0) * x
        return carry

    lax.fori_loop(0, 8, step, 0)


def two_planes(z_ref, n):
    return split(jnp.concatenate([z_ref[2 * n], z_ref[2 * n + 1]], axis=1))


def along_y(z_ref, out_ref, kl_ref):
    def step(n, carry):
        high, low = two_planes(z_ref, n)
        res = mm(kl_ref[...], jnp.concatenate([high, low, high], axis=0))
        out_ref[2 * n] = res[:, :128]
        out_ref[2 * n + 1] = res[:, 128:]
        return carry

    lax.fori_loop(0, 4, step, 0)


def build_frames(at_ref, frames, rows_f32, pick, pick_t, marks_ref):
    first_plane = (8 * index_of(BLOCK)).astype(F32)
    first_col = (128 * lax.axis_index("core")).astype(F32)
    dz, dx = marks_ref[128:129, :], marks_ref[129:130, :]

    def step(a, carry):
        slot, i = a // 16, lax.rem(a, 16)
        meta = at_ref[slot, pl.ds(64 + i, 1), :]
        plane = wrapped(meta[:, 0:1] + dz) - first_plane
        col = wrapped(meta[:, 2:3] + dx) - first_col
        mask = jnp.where(plane == marks_ref[0:64, :], marks_ref[64:128, :], 0.0)
        parts = []
        for p in range(4):
            parts.append(mask * at_ref[slot, pl.ds(4 * i + p, 1), :])
        high, low = split(jnp.concatenate(parts, axis=0))
        cols = lax.broadcasted_iota(jnp.int32, (128, 128), 0).astype(F32)
        hit = jnp.where(cols == col, 1.0, 0.0).astype(jnp.bfloat16)
        res = mm_nt(high, hit) + mm_nt(low, hit)
        at = pl.ds(pl.multiple_of(8 * a, 8), 8)
        for p in range(4):
            for z in range(8):
                frames[z, p, at, :] = res[64 * p + 8 * z : 64 * p + 8 * z + 8]
        row = wrapped(meta[:, 1:2] + lax.broadcasted_iota(jnp.int32, (8, 1), 0).astype(F32) - 3.0)
        ys = lax.broadcasted_iota(jnp.int32, (8, N), 1).astype(F32)
        rows_f32[at, :] = jnp.where(ys == row, 1.0, 0.0)
        return carry

    lax.fori_loop(0, 64, step, 0)
    pick[...] = rows_f32[...].astype(jnp.bfloat16)
    ys = lax.broadcasted_iota(jnp.int32, (N, 128), 0).astype(F32)
    for slot in range(4):
        pick_t[:, 128 * slot : 128 * slot + 128] = jnp.where(
            ys == at_ref[slot, 80:81, :], 1.0, 0.0
        ).astype(jnp.bfloat16)


def project(z_ref, picked, frames, pick, part):
    def rows(n, carry):
        high, low = two_planes(z_ref, n)
        res = mm(pick[...], high) + mm(pick[...], low)
        picked[2 * n] = res[:, :128]
        picked[2 * n + 1] = res[:, 128:]
        return carry

    lax.fori_loop(0, 4, rows, 0)
    lanes = lax.broadcasted_iota(jnp.int32, (8, 128), 1)

    def atoms(n, carry):
        at = pl.ds(pl.multiple_of(64 * n, 64), 64)
        sums = [jnp.zeros((64, 128), F32) for _ in range(4)]
        for z in range(8):
            field = picked[z, at, :]
            for p in range(4):
                sums[p] = sums[p] + frames[z, p, at, :] * field
        value = jnp.zeros((8, 128), F32)
        for p in range(4):
            total = jnp.sum(jnp.sum(sums[p].reshape(8, 8, 128), axis=1), axis=1, keepdims=True)
            value = jnp.where(lanes == p, total, value)
        part[pl.ds(pl.multiple_of(8 * n, 8), 8), :] = value
        return carry

    lax.fori_loop(0, 8, atoms, 0)


def spread_back(coeffs, picked, frames, pick_t, out_ref):
    def atoms(n, carry):
        value = coeffs[pl.ds(pl.multiple_of(8 * n, 8), 8), :]
        for i in range(8):
            at = pl.ds(pl.multiple_of(64 * n + 8 * i, 8), 8)
            wide = [jnp.broadcast_to(value[i : i + 1, p : p + 1], (8, 128)) for p in range(4)]
            for z in range(8):
                total = wide[0] * frames[z, 0, at, :]
                for p in range(1, 4):
                    total = total + wide[p] * frames[z, p, at, :]
                picked[z, at, :] = total
        return carry

    lax.fori_loop(0, 8, atoms, 0)

    def planes(n, carry):
        high, low = two_planes(picked, n)
        res = mm(pick_t[...], high) + mm(pick_t[...], low)
        out_ref[2 * n] += res[:, :128]
        out_ref[2 * n + 1] += res[:, 128:]
        return carry

    lax.fori_loop(0, 4, planes, 0)


def copy_to(src, dst, send, recv, coords):
    return pltpu.make_async_remote_copy(
        src_ref=src, dst_ref=dst, send_sem=send, recv_sem=recv, device_id=coords, device_id_type=MESH
    )


class Swap:
    def __init__(self, axes, source, target, send, recv):
        self.args = (axes, source, target, send, recv)

    def start(self):
        swap_start(*self.args)

    def wait(self):
        swap_wait(*self.args)


def planes_swap(y_ref, z_ref, send, recv):
    return Swap(
        BLOCK,
        lambda peer: y_ref.at[pl.ds(pl.multiple_of(peer * 8, 8), 8)],
        lambda peer: z_ref.at[:, pl.ds(pl.multiple_of(peer * 8, 8), 8), :],
        send,
        recv,
    )


def rows_swap(z_ref, y_ref, send, recv):
    return Swap(
        BLOCK,
        lambda peer: z_ref.at[:, pl.ds(pl.multiple_of(peer * 8, 8), 8), :],
        lambda peer: y_ref.at[pl.ds(pl.multiple_of(peer * 8, 8), 8)],
        send,
        recv,
    )


class Coeffs:
    def __init__(self, part, got, send, recv):
        core, me = lax.axis_index("core"), index_of(BLOCK)
        up, down = lax.rem(me + 1, 32), lax.rem(me + 31, 32)
        low, high = pl.ds(0, 32), pl.ds(32, 32)

        def place(chip, which):
            coords = coords_of(BLOCK, chip)
            coords["core"] = which
            return coords

        other = {"core": 1 - core}
        self.coords = [other]
        self.copies = [copy_to(part.at[low], got.at[0], send.at[0], recv.at[0], other)]
        self.copies.append(copy_to(part.at[high], got.at[1], send.at[1], recv.at[1], other))
        for n in range(2):
            which = lax.rem(core + n, 2)
            above, below = place(up, which), place(down, which)
            self.coords += [above, below]
            slot = 2 + core
            self.copies.append(copy_to(part.at[high], got.at[slot], send.at[2 + n], recv.at[slot], above))
            slot = 4 + core
            self.copies.append(copy_to(part.at[low], got.at[slot], send.at[4 + n], recv.at[slot], below))
        self.arrivals = [
            copy_to(part.at[low], got.at[slot], send.at[0], recv.at[slot], other) for slot in range(6)
        ]

    def greet(self, barrier):
        for coords in self.coords:
            pl.semaphore_signal(barrier, inc=1, device_id=coords, device_id_type=MESH)
        return len(self.coords)

    def start(self):
        for copy in self.copies:
            copy.start()

    def wait(self):
        for copy in self.copies:
            copy.wait_send()
        for copy in self.arrivals:
            copy.wait_recv()


def filter_block(
    cheb_ref, kb_ref, v_ref, pot_ref, at_ref, kl_ref, kr_ref, marks_ref, out_ref,
    planes, sibs, backs, first, in_rows, in_planes, frames, picked, rows_f32, pick, pick_t, part, got, coeffs,
    zsend, zrecv, ysend, yrecv, ssend, srecv, csend, crecv,
):
    core = lax.axis_index("core")
    barrier, greeted = greet_group(BLOCK)
    shares = [Coeffs(part.at[n], got.at[n], csend.at[n], crecv.at[n]) for n in range(2)]
    greeted = greeted + shares[0].greet(barrier)
    pl.semaphore_wait(barrier, greeted)

    for n in range(2):
        x_ref = v_ref if n == 0 else first
        out = planes_swap(x_ref, planes.at[n], zsend.at[n], zrecv.at[n])
        sib = copy_to(x_ref, sibs.at[n], ssend.at[n], srecv.at[n], {"core": 1 - core})
        out.start()
        sib.start()
        along_z(x_ref, in_rows, kl_ref)
        if n == 0:
            build_frames(at_ref, frames, rows_f32, pick, pick_t, marks_ref)
        sib.wait()
        along_x(x_ref, sibs.at[n], pot_ref, in_rows, kr_ref)
        out.wait()
        share = shares[n]
        project(planes.at[n], picked, frames, pick, part.at[n])
        share.start()
        along_y(planes.at[n], in_planes.at[n], kl_ref)
        share.wait()
        low, high = pl.ds(0, 32), pl.ds(32, 32)
        own, them = part.at[n], got.at[n]
        coeffs[low, :] = (own[low, :] + them[0] + them[2] + them[3]) * kb_ref[...]
        coeffs[high, :] = (own[high, :] + them[1] + them[4] + them[5]) * kb_ref[...]
        spread_back(coeffs, picked, frames, pick_t, in_planes.at[n])
        back = rows_swap(in_planes.at[n], backs.at[n], ysend.at[n], yrecv.at[n])
        back.start()
        back.wait()
        if n == 0:
            def sum_up(k, carry):
                zs = pl.ds(k * 32, 32)
                first[zs] = (backs[0, zs] + in_rows[zs]) * 0.25
                return carry
        else:
            def sum_up(k, carry):
                zs = pl.ds(k * 32, 32)
                second = 0.5 * (backs[1, zs] + in_rows[zs]) - v_ref[zs]
                value = cheb_ref[0] * v_ref[zs] + cheb_ref[1] * first[zs] + cheb_ref[2] * second
                out_ref[zs] = value * value
                return carry

        lax.fori_loop(0, 8, sum_up, 0)


def filter_call(cheb, kb, v, pot, atoms):
    table = kinetic_table(N)
    high, low = split3(table)
    left = np.concatenate([high, high, low], axis=1)
    side = np.concatenate([table[:128, :128], table[128:, :128]], axis=0)
    high, low = split3(side)
    right = np.concatenate([high, high, low], axis=0)
    off = sphere_offsets()
    marks = np.zeros((136, 128), np.float32)
    rows = np.arange(64)[:, None]
    marks[:64] = rows // 8
    marks[64:128] = off[None, :, 1] + REACH == rows % 8
    marks[128] = off[:, 0]
    marks[129] = off[:, 2]
    kb_row = jnp.pad(kb, (0, 124)).reshape(1, 128)
    field = (N, 8, 128)
    slab = (8, N, 128)
    vmem = pl.BlockSpec(memory_space=pltpu.VMEM)
    bf16 = jnp.bfloat16
    return pl.pallas_call(
        filter_block,
        out_shape=jax.ShapeDtypeStruct(field, F32),
        in_specs=[pl.BlockSpec(memory_space=pltpu.SMEM)] + [vmem] * 7,
        out_specs=vmem,
        scratch_shapes=[
            pltpu.VMEM((2,) + slab, F32),
            pltpu.VMEM((2,) + field, F32),
            pltpu.VMEM((2,) + field, F32),
            pltpu.VMEM(field, F32),
            pltpu.VMEM(field, F32),
            pltpu.VMEM((2,) + slab, F32),
            pltpu.VMEM((8, 4, 512, 128), F32),
            pltpu.VMEM((8, 512, 128), F32),
            pltpu.VMEM((512, N), F32),
            pltpu.VMEM((512, N), bf16),
            pltpu.VMEM((N, 512), bf16),
            pltpu.VMEM((2, 64, 128), F32),
            pltpu.VMEM((2, 6, 32, 128), F32),
            pltpu.VMEM((64, 128), F32),
            dma(2, 32), dma(2, 32), dma(2, 32), dma(2, 32), dma(2), dma(2), dma(2, 6), dma(2, 6),
        ],
        compiler_params=pltpu.CompilerParams(
            collective_id=4, has_side_effects=True, vmem_limit_bytes=48 * 1024 * 1024
        ),
    )(cheb, kb_row, v, pot, atoms, left, right, marks)


def local(random_orbitals, potential, sphere_cells, projectors, kb_energy, cheb_coef):
    v_rows, pot_rows = comm_call(
        spread_rows, 1, [(16, 4, 16, N), (2, 4, 16, N)], [dma(16), dma(16), dma(1), dma(2)],
        random_orbitals[0], potential,
    )
    v, pot = comm_call(
        spread_planes, 2, [(2, 32, 4, 8, 128)] * 2, [dma(32)] * 4,
        v_rows.reshape(8, 2, 4, 16, N), pot_rows,
    )
    v, pot = v.reshape(N, 8, 128), pot.reshape(N, 8, 128)

    lanes = lax.broadcasted_iota(jnp.int32, (16, 128), 1)
    centre_z, cell = sphere_cells[:, 0, :1], sphere_cells[:, 1, :1]
    centre_y, centre_x = cell // N, cell % N
    meta = jnp.where(lanes == 0, centre_z, jnp.where(lanes == 1, centre_y, centre_x))
    hit_rows = (centre_y + jnp.arange(8)[None, :] - REACH) % N
    extra = jnp.broadcast_to(hit_rows.reshape(1, 128), (8, 128))
    packed = jnp.concatenate([projectors.reshape(64, SPH), meta.astype(F32), extra.astype(F32)], axis=0)
    (atoms,) = comm_call(spread_atoms, 3, [(4, 88, 128)], [dma(4), dma(4)], packed)

    squares = filter_call(cheb_coef, kb_energy, v, pot, atoms).reshape(2, 8, 16, 8, 128)
    (parts,) = comm_call(gather_squares, 7, [(8, 2, 16, 8, 128)], [dma(8), dma(8)], squares)
    summed = (jnp.sum(parts, axis=0) / 8.0).reshape(2, 2, 2, 4, 8, 128)
    (density,) = comm_call(place_density, 8, [(4, N, N)], [dma(64), dma(64)], summed)
    return density


def solution(mesh):
    apart = Mesh(mesh.devices.reshape([SIZES[name] for name in AXES]), AXES)
    orb, grid = ("y", "xl"), ("xh", "zb", "par", "core")
    in_specs = (P(orb, grid), P(grid), P(grid), P(grid), P(), P())
    return jax.shard_map(local, mesh=apart, in_specs=in_specs, out_specs=P(grid), check_vma=False)
```

```python
import functools

import jax
import jax.numpy as jnp
import numpy as np
from jax import lax
from jax.experimental import pallas as pl
from jax.experimental.pallas import tpu as pltpu
from jax.sharding import Mesh, PartitionSpec as P

AXES = ("y", "xl", "xh", "zb", "par", "core")
SIZES = {"y": 4, "xl": 2, "xh": 2, "zb": 8, "par": 2, "core": 2}
PLANE = ("y", "xl", "xh")
LINE = ("zb", "par", "core")
BLOCK = ("y", "xl", "xh", "par")
QUAD = ("y", "xl", "xh", "par", "core")

N = 256
REACH = 3
SPH = 128
MESH = pl.DeviceIdType.MESH
F32 = jnp.float32


def kinetic_table(length):
    places = np.arange(length)
    offset = places[:, None] - places[None, :]
    parity = np.where(offset % 2 == 0, 1.0, -1.0)
    sine = np.where(offset == 0, 1.0, np.sin(offset * (np.pi / length)))
    table = np.where(offset == 0, length * length / 12.0 + 1.0 / 6.0, parity / (2.0 * sine * sine))
    return (table * (4.0 / (length * length))).astype(np.float32)


def sphere_offsets():
    width = 2 * REACH + 1
    count = width**3
    ids = np.arange(count)
    off = np.stack([ids // (width * width), ids // width % width, ids % width], axis=1) - REACH
    radius = (off * off).sum(axis=1)
    return off[np.argsort(radius * count + ids, kind="stable")[:SPH]]


def index_of(axes):
    where = 0
    for name in axes:
        where = where * SIZES[name] + lax.axis_index(name)
    return where


def coords_of(axes, where):
    coords = {}
    for name in reversed(axes):
        coords[name] = lax.rem(where, SIZES[name])
        where = where // SIZES[name]
    return coords


def group_size(axes):
    return int(np.prod([SIZES[name] for name in axes]))


def greet_group(axes):
    me, count = index_of(axes), group_size(axes)
    barrier = pltpu.get_barrier_semaphore()

    def greet(k, carry):
        pl.semaphore_signal(
            barrier, inc=1, device_id=coords_of(axes, lax.rem(me + k, count)), device_id_type=MESH
        )
        return carry

    lax.fori_loop(1, count, greet, 0)
    return barrier, count - 1


def swap_start(axes, source, target, send, recv):
    me, count = index_of(axes), group_size(axes)

    def step(k, carry):
        peer = lax.rem(me + k, count)
        pltpu.make_async_remote_copy(
            src_ref=source(peer),
            dst_ref=target(me),
            send_sem=send.at[peer],
            recv_sem=recv.at[me],
            device_id=coords_of(axes, peer),
            device_id_type=MESH,
        ).start()
        return carry

    lax.fori_loop(1, count, step, 0)
    pltpu.make_async_copy(source(me), target(me), recv.at[me]).start()


def swap_wait(axes, source, target, send, recv):
    me, count = index_of(axes), group_size(axes)

    def step(k, carry):
        peer = lax.rem(me + k, count)
        copy = pltpu.make_async_remote_copy(
            src_ref=source(peer),
            dst_ref=target(peer),
            send_sem=send.at[peer],
            recv_sem=recv.at[peer],
            device_id=coords_of(axes, peer),
            device_id_type=MESH,
        )
        copy.wait_send()
        copy.wait_recv()
        return carry

    lax.fori_loop(1, count, step, 0)
    pltpu.make_async_copy(source(me), target(me), recv.at[me]).wait()


def copy_to(src, dst, send, recv, coords):
    return pltpu.make_async_remote_copy(
        src_ref=src, dst_ref=dst, send_sem=send, recv_sem=recv, device_id=coords, device_id_type=MESH
    )


def dma(*shape):
    return pltpu.SemaphoreType.DMA(shape)


def home_of(orbital, slab):
    return {
        "y": orbital // 2,
        "xl": lax.rem(orbital, 2),
        "xh": slab // 32,
        "zb": lax.rem(slab // 4, 8),
        "par": lax.rem(slab // 2, 2),
        "core": lax.rem(slab, 2),
    }


def full(coords):
    return tuple(coords[name] for name in AXES)


def is_me(coords):
    same = coords["y"] == lax.axis_index("y")
    for name in AXES[1:]:
        same = jnp.logical_and(same, coords[name] == lax.axis_index(name))
    return same


class Atoms:
    def __init__(self, at_ref, at_out, send, recv):
        slab = index_of(("xh", "zb", "par", "core"))
        orbital = index_of(("y", "xl"))
        odd = lax.rem(slab, 2)
        chip, near = slab // 2, lax.rem(slab // 2 + 2 * odd - 1 + 32, 32)
        mine, zb = index_of(BLOCK), lax.axis_index("zb")
        self.refs = (at_ref, at_out, send, recv)
        self.homes = [home_of(zb, lax.rem(2 * mine - 1 + slot + 64, 64)) for slot in range(4)]
        self.sends = []
        for n, (q, slot) in enumerate(((chip, 1 + odd), (near, 3 - 3 * odd))):
            for core in range(2):
                place = coords_of(BLOCK, q)
                place["zb"] = orbital
                place["core"] = jnp.int32(core)
                self.sends.append((place, slot, 2 * n + core))

    def greet(self, barrier):
        own = jnp.int32(0)
        for home in self.homes:
            same = is_me(home)
            own = own + same.astype(jnp.int32)

            @pl.when(jnp.logical_not(same))
            def _():
                pl.semaphore_signal(barrier, inc=1, device_id=full(home), device_id_type=MESH)

        return 4 - own

    def each(self, go):
        at_ref, at_out, send, recv = self.refs
        for place, slot, n in self.sends:
            same = is_me(place)

            @pl.when(jnp.logical_not(same))
            def _():
                copy = copy_to(at_ref, at_out.at[slot], send.at[n], recv.at[slot], full(place))
                if go:
                    copy.start()
                else:
                    copy.wait_send()

            @pl.when(same)
            def _():
                copy = pltpu.make_async_copy(at_ref, at_out.at[slot], send.at[n])
                if go:
                    copy.start()
                else:
                    copy.wait()

    def start(self):
        self.each(True)

    def wait(self):
        at_ref, at_out, send, recv = self.refs
        self.each(False)
        for slot, home in enumerate(self.homes):
            @pl.when(jnp.logical_not(is_me(home)))
            def _():
                copy_to(at_ref, at_out.at[slot], send.at[0], recv.at[slot], full(home)).wait_recv()


def split3(table):
    high = table.astype(jnp.bfloat16)
    low = (table - high.astype(np.float32)).astype(jnp.bfloat16)
    return high, low


def split(x):
    high = x.astype(jnp.bfloat16)
    return high, (x - high.astype(F32)).astype(jnp.bfloat16)


def mm(a, b):
    return lax.dot_general(a, b, (((1,), (0,)), ((), ())), preferred_element_type=F32)


def mm_nt(a, b):
    return lax.dot_general(a, b, (((1,), (1,)), ((), ())), preferred_element_type=F32)


def wrapped(x):
    x = jnp.where(x < 0.0, x + 256.0, x)
    return jnp.where(x > 255.0, x - 256.0, x)


def along_z(x_ref, out_ref, kl_ref):
    table = kl_ref[...]
    for pair in range(4):
        x = jnp.concatenate(
            [x_ref[:, :, 2 * pair, :].reshape(N, 128), x_ref[:, :, 2 * pair + 1, :].reshape(N, 128)], axis=1
        )
        high, low = split(x)
        res = mm(table, jnp.concatenate([high, low, high], axis=0))
        out_ref[:, :, 2 * pair, :] = res[:, :128].reshape(2, 128, 128)
        out_ref[:, :, 2 * pair + 1, :] = res[:, 128:].reshape(2, 128, 128)


def planes_at(n):
    return n // 4, pl.ds(pl.multiple_of(lax.rem(n, 4) * 32, 32), 32)


def along_x(x_ref, sib_ref, out_ref, kr_ref):
    def step(n, carry):
        half, zs = planes_at(n)
        x = x_ref[half, zs]
        both = jnp.concatenate([x.reshape(256, 128), sib_ref[half, zs].reshape(256, 128)], axis=1)
        high, low = split(both)
        res = mm(jnp.concatenate([high, low, high], axis=1), kr_ref[...])
        out_ref[half, zs] += res.reshape(32, 8, 128) - 2.0 * x
        return carry

    lax.fori_loop(0, 8, step, 0)


def two_planes(z_ref, n):
    return split(jnp.concatenate([z_ref[2 * n], z_ref[2 * n + 1]], axis=1))


def along_y(z_ref, out_ref, kl_ref):
    def step(n, carry):
        high, low = two_planes(z_ref, n)
        res = mm(kl_ref[...], jnp.concatenate([high, low, high], axis=0))
        out_ref[2 * n] = res[:, :128]
        out_ref[2 * n + 1] = res[:, 128:]
        return carry

    lax.fori_loop(0, 4, step, 0)


def build_frames(at_ref, frames, rows_f32, pick, pick_t, marks_ref):
    first_plane = (8 * index_of(BLOCK)).astype(F32)
    first_col = (128 * lax.axis_index("core")).astype(F32)
    dz, dx = marks_ref[128:129, :], marks_ref[129:130, :]

    def step(a, carry):
        slot, i = a // 16, lax.rem(a, 16)
        meta = at_ref[slot, pl.ds(64 + i, 1), :]
        plane = wrapped(meta[:, 0:1] + dz) - first_plane
        col = wrapped(meta[:, 2:3] + dx) - first_col
        mask = jnp.where(plane == marks_ref[0:64, :], marks_ref[64:128, :], 0.0)
        parts = []
        for p in range(4):
            parts.append(mask * at_ref[slot, pl.ds(4 * i + p, 1), :])
        high, low = split(jnp.concatenate(parts, axis=0))
        cols = lax.broadcasted_iota(jnp.int32, (128, 128), 0).astype(F32)
        hit = jnp.where(cols == col, 1.0, 0.0).astype(jnp.bfloat16)
        res = mm_nt(high, hit) + mm_nt(low, hit)
        at = pl.ds(pl.multiple_of(8 * a, 8), 8)
        for p in range(4):
            for z in range(8):
                frames[z, p, at, :] = res[64 * p + 8 * z : 64 * p + 8 * z + 8]
        row = wrapped(meta[:, 1:2] + lax.broadcasted_iota(jnp.int32, (8, 1), 0).astype(F32) - 3.0)
        ys = lax.broadcasted_iota(jnp.int32, (8, N), 1).astype(F32)
        rows_f32[at, :] = jnp.where(ys == row, 1.0, 0.0)
        return carry

    lax.fori_loop(0, 64, step, 0)
    pick[...] = rows_f32[...].astype(jnp.bfloat16)
    ys = lax.broadcasted_iota(jnp.int32, (N, 128), 0).astype(F32)
    for slot in range(4):
        pick_t[:, 128 * slot : 128 * slot + 128] = jnp.where(
            ys == at_ref[slot, 80:81, :], 1.0, 0.0
        ).astype(jnp.bfloat16)


def project(z_ref, picked, frames, pick, part):
    def rows(n, carry):
        high, low = two_planes(z_ref, n)
        res = mm(pick[...], high) + mm(pick[...], low)
        picked[2 * n] = res[:, :128]
        picked[2 * n + 1] = res[:, 128:]
        return carry

    lax.fori_loop(0, 4, rows, 0)
    lanes = lax.broadcasted_iota(jnp.int32, (8, 128), 1)

    def atoms(n, carry):
        at = pl.ds(pl.multiple_of(64 * n, 64), 64)
        sums = [jnp.zeros((64, 128), F32) for _ in range(4)]
        for z in range(8):
            field = picked[z, at, :]
            for p in range(4):
                sums[p] = sums[p] + frames[z, p, at, :] * field
        value = jnp.zeros((8, 128), F32)
        for p in range(4):
            total = jnp.sum(jnp.sum(sums[p].reshape(8, 8, 128), axis=1), axis=1, keepdims=True)
            value = jnp.where(lanes == p, total, value)
        part[pl.ds(pl.multiple_of(8 * n, 8), 8), :] = value
        return carry

    lax.fori_loop(0, 8, atoms, 0)


def spread_back(coeffs, picked, frames, pick_t, out_ref):
    def atoms(n, carry):
        value = coeffs[pl.ds(pl.multiple_of(8 * n, 8), 8), :]
        for i in range(8):
            at = pl.ds(pl.multiple_of(64 * n + 8 * i, 8), 8)
            wide = [jnp.broadcast_to(value[i : i + 1, p : p + 1], (8, 128)) for p in range(4)]
            for z in range(8):
                total = wide[0] * frames[z, 0, at, :]
                for p in range(1, 4):
                    total = total + wide[p] * frames[z, p, at, :]
                picked[z, at, :] = total
        return carry

    lax.fori_loop(0, 8, atoms, 0)

    def planes(n, carry):
        high, low = two_planes(picked, n)
        res = mm(pick_t[...], high) + mm(pick_t[...], low)
        out_ref[2 * n] += res[:, :128]
        out_ref[2 * n + 1] += res[:, 128:]
        return carry

    lax.fori_loop(0, 4, planes, 0)


class Swap:
    def __init__(self, axes, source, target, send, recv):
        self.axes, self.source, self.target, self.send, self.recv = axes, source, target, send, recv
        self.me = index_of(axes)

    def remote(self, peer, arriving):
        return copy_to(
            self.source(peer),
            self.target(peer if arriving else self.me),
            self.send.at[peer],
            self.recv.at[peer if arriving else self.me],
            coords_of(self.axes, peer),
        )

    def own(self):
        return pltpu.make_async_copy(self.source(self.me), self.target(self.me), self.recv.at[self.me])

    def start(self):
        swap_start(self.axes, self.source, self.target, self.send, self.recv)

    def wait(self):
        swap_wait(self.axes, self.source, self.target, self.send, self.recv)

    def start_one(self, peer):
        @pl.when(peer != self.me)
        def _():
            self.remote(peer, False).start()

        @pl.when(peer == self.me)
        def _():
            self.own().start()

    def wait_arrival(self, peer):
        @pl.when(peer != self.me)
        def _():
            self.remote(peer, True).wait_recv()

        @pl.when(peer == self.me)
        def _():
            self.own().wait()

    def wait_sends(self):
        count = group_size(self.axes)

        def step(k, carry):
            self.remote(lax.rem(self.me + k, count), True).wait_send()
            return carry

        lax.fori_loop(1, count, step, 0)


def planes_of(field, q):
    return field.at[q // 16, pl.ds(pl.multiple_of(lax.rem(q, 16) * 8, 8), 8)]


def planes_swap(y_ref, z_ref, send, recv):
    return Swap(
        BLOCK,
        lambda peer: planes_of(y_ref, peer),
        lambda peer: z_ref.at[:, pl.ds(pl.multiple_of(peer * 8, 8), 8), :],
        send,
        recv,
    )


def rows_swap(z_ref, y_ref, send, recv):
    return Swap(
        BLOCK,
        lambda peer: z_ref.at[:, pl.ds(pl.multiple_of(peer * 8, 8), 8), :],
        lambda peer: planes_of(y_ref, peer),
        send,
        recv,
    )


def tile_at(rows, cols):
    return pl.ds(pl.multiple_of(rows * 8, 8), 8), pl.ds(pl.multiple_of(cols * 128, 128), 128)


class Ring:
    def __init__(self, ring, send, recv):
        self.refs = (ring, send, recv)
        self.z = index_of(("zb", "par"))
        self.steps = (8, 7)

    def copy(self, way, step):
        ring, send, recv = self.refs
        turn = 1 if way == 0 else 15
        slot = lax.rem(self.z + (16 - step if way == 0 else step), 16)
        return copy_to(
            ring.at[:, slot],
            ring.at[:, slot],
            send.at[way, step],
            recv.at[way, step],
            coords_of(("zb", "par"), lax.rem(self.z + turn, 16)),
        )

    def arrival(self, way, step):
        ring, send, recv = self.refs
        slot = lax.rem(self.z + (15 - step if way == 0 else step + 1), 16)
        turn = 1 if way == 0 else 15
        return copy_to(
            ring.at[:, slot],
            ring.at[:, slot],
            send.at[way, step],
            recv.at[way, step],
            coords_of(("zb", "par"), lax.rem(self.z + turn, 16)),
        )

    def step(self, step):
        for way in range(2):
            if 0 < step <= self.steps[way]:
                self.arrival(way, step - 1).wait_recv()
            if step < self.steps[way]:
                self.copy(way, step).start()

    def wait_sends(self):
        for way in range(2):
            for step in range(self.steps[way]):
                self.copy(way, step).wait_send()


class Coeffs:
    def __init__(self, part, got, send, recv):
        core, me = lax.axis_index("core"), index_of(BLOCK)
        up, down = lax.rem(me + 1, 32), lax.rem(me + 31, 32)
        low, high = pl.ds(0, 32), pl.ds(32, 32)

        def place(chip, which):
            coords = coords_of(BLOCK, chip)
            coords["core"] = which
            return coords

        other = {"core": 1 - core}
        self.coords = [other]
        self.copies = [copy_to(part.at[low], got.at[0], send.at[0], recv.at[0], other)]
        self.copies.append(copy_to(part.at[high], got.at[1], send.at[1], recv.at[1], other))
        for n in range(2):
            which = lax.rem(core + n, 2)
            above, below = place(up, which), place(down, which)
            self.coords += [above, below]
            slot = 2 + core
            self.copies.append(copy_to(part.at[high], got.at[slot], send.at[2 + n], recv.at[slot], above))
            slot = 4 + core
            self.copies.append(copy_to(part.at[low], got.at[slot], send.at[4 + n], recv.at[slot], below))
        self.arrivals = [
            copy_to(part.at[low], got.at[slot], send.at[0], recv.at[slot], other) for slot in range(6)
        ]

    def greet(self, barrier):
        for coords in self.coords:
            pl.semaphore_signal(barrier, inc=1, device_id=coords, device_id_type=MESH)
        return len(self.coords)

    def start(self):
        for copy in self.copies:
            copy.start()

    def wait(self):
        for copy in self.copies:
            copy.wait_send()
        for copy in self.arrivals:
            copy.wait_recv()


def sum_squares(squares, sums, total, send, recv):
    zb = lax.axis_index("zb")
    eight = pl.ds(0, 8)

    def flow(way, half, step):
        turn = 1 if way == 0 else 7
        place = {"zb": lax.rem(zb + turn, 8)}
        dst = sums.at[way, half, step]
        return place, dst, send.at[way, half, step], recv.at[way, half, step]

    def own(way, half, away):
        chunk = lax.rem(zb + (16 - away if way == 0 else away), 8)
        return way, pl.ds(pl.multiple_of(chunk * 16 + half * 8, 8), 8)

    flows = [(way, half) for half in range(2) for way in range(2)]
    for way, half in flows:
        place, dst, one, two = flow(way, half, 0)
        copy_to(squares.at[own(way, half, 1)], dst, one, two, place).start()

    def step(n, carry):
        for way, half in flows:
            place, dst, one, two = flow(way, half, n)
            before, src, was_one, was_two = flow(way, half, n - 1)
            copy_to(src, src, was_one, was_two, before).wait_recv()
            sums[way, half, n - 1] += squares[own(way, half, n + 1)]
            copy_to(src, dst, one, two, place).start()
        return carry

    lax.fori_loop(1, 7, step, 0)
    for way, half in flows:
        place, dst, one, two = flow(way, half, 6)
        copy_to(dst, dst, one, two, place).wait_recv()
        total[way, 8 * half : 8 * half + 8] = (sums[way, half, 6] + squares[own(way, half, 0)]) * 0.125

    def finish(n, carry):
        for way, half in flows:
            place, dst, one, two = flow(way, half, n)
            copy_to(dst, dst, one, two, place).wait_send()
        return carry

    lax.fori_loop(0, 7, finish, 0)


def program(
    cheb_ref, kb_ref, orbital_ref, pot_ref, packed_ref, kl_ref, kr_ref, marks_ref, out_ref,
    v_rows, v, ring_ref, atoms, planes, sibs, backs, first, in_rows, in_planes, frames, picked, rows_f32,
    pick, pick_t, part, got, coeffs, sums, total,
    asend, arecv, rsend, rrecv, lsend, lrecv, psend, precv, vsend, vrecv,
    zsend, zrecv, ysend, yrecv, ssend, srecv, csend, crecv, qsend, qrecv, dsend, drecv,
):
    core, par, zb, xh = (lax.axis_index(name) for name in ("core", "par", "zb", "xh"))
    plane_me = index_of(PLANE)
    z_me = 2 * zb + par
    barrier, greeted = greet_group(QUAD)
    greeted = greeted + greet_group(LINE)[1]
    spread = Atoms(packed_ref, atoms, asend, arecv)
    greeted = greeted + spread.greet(barrier)
    pl.semaphore_wait(barrier, greeted)

    to_owner = Swap(
        PLANE,
        lambda peer: orbital_ref.at[:, pl.ds(pl.multiple_of(peer * 16, 16), 16), :],
        lambda peer: v_rows.at[peer],
        rsend,
        rrecv,
    )
    pot_owner = Swap(
        ("xh", "core"),
        lambda peer: pot_ref.at[
            :,
            pl.ds(pl.multiple_of((plane_me - xh + peer // 2) * 16, 16), 16),
            pl.ds(pl.multiple_of(lax.rem(peer, 2) * 128, 128), 128),
        ],
        lambda peer: ring_ref.at[peer // 2, z_me, pl.ds(pl.multiple_of(lax.rem(peer, 2) * 4, 4), 4)],
        psend,
        precv,
    )
    ring = Ring(ring_ref, vsend, vrecv)
    pot_owner.start()
    to_owner.start()
    spread.start()
    pot_owner.wait()
    ring.step(0)

    def line_source(peer):
        rows, cols = tile_at(lax.rem(peer // 2, 2), lax.rem(peer, 2))
        return v_rows.at[pl.ds(peer // 4 * 2, 2), :, rows, cols]

    line = Swap(
        LINE, line_source, lambda peer: v.at[:, pl.ds(pl.multiple_of(peer * 4, 4), 4)], lsend, lrecv
    )

    def to_block(k, carry):
        there = lax.rem(zb + k, 8)
        to_owner.wait_arrival(2 * there)
        to_owner.wait_arrival(2 * there + 1)
        for n in range(4):
            line.start_one(4 * there + n)
        return carry

    lax.fori_loop(0, 8, to_block, 0)
    ring.step(1)
    spread.wait()
    build_frames(atoms, frames, rows_f32, pick, pick_t, marks_ref)

    out = planes_swap(v, planes.at[0], zsend.at[0], zrecv.at[0])

    def arrive(k, carry):
        there = lax.rem(zb - k + 8, 8)
        for n in range(4):
            line.wait_arrival(4 * there + n)
            if n % 2 == 1:
                z = 2 * there + n // 2
                out.start_one(z)
                out.start_one(16 + z)
        return carry

    for n in range(4):
        lax.fori_loop(2 * n, 2 * n + 2, arrive, 0)
        if n < 3:
            ring.step(2 + n)

    shares = [Coeffs(part.at[n], got.at[n], csend.at[n], crecv.at[n]) for n in range(2)]

    def pot_at(half, n):
        zs = pl.ds(pl.multiple_of(lax.rem(n, 4) * 4, 4), 4)
        rows = pl.ds(pl.multiple_of(par * 8, 8), 8)
        return ring_ref[half, zs, :, rows, :].reshape(32, 8, 128)

    for n in range(2):
        x_ref = v if n == 0 else first
        sib = copy_to(x_ref, sibs.at[n], ssend.at[n], srecv.at[n], {"core": 1 - core})
        if n == 1:
            out = planes_swap(x_ref, planes.at[n], zsend.at[n], zrecv.at[n])
            out.start()
        sib.start()
        along_z(x_ref, in_rows, kl_ref)
        if n == 0:
            ring.step(5)
        sib.wait()
        along_x(x_ref, sibs.at[n], in_rows, kr_ref)
        out.wait()
        share = shares[n]
        project(planes.at[n], picked, frames, pick, part.at[n])
        share.start()
        if n == 0:
            ring.step(6)
        along_y(planes.at[n], in_planes.at[n], kl_ref)
        share.wait()
        low, high = pl.ds(0, 32), pl.ds(32, 32)
        own, them = part.at[n], got.at[n]
        coeffs[low, :] = (own[low, :] + them[0] + them[2] + them[3]) * kb_ref[...]
        coeffs[high, :] = (own[high, :] + them[1] + them[4] + them[5]) * kb_ref[...]
        spread_back(coeffs, picked, frames, pick_t, in_planes.at[n])
        back = rows_swap(in_planes.at[n], backs.at[n], ysend.at[n], yrecv.at[n])
        back.start()
        if n == 0:
            ring.step(7)
            ring.step(8)
        back.wait()

        if n == 0:
            def sum_up(k, carry):
                half, zs = planes_at(k)
                x = v[half, zs]
                first[half, zs] = (backs[0, half, zs] + in_rows[half, zs] + pot_at(half, k) * x) * 0.25
                return carry
        else:
            def sum_up(k, carry):
                half, zs = planes_at(k)
                x, one = v[half, zs], first[half, zs]
                second = 0.5 * (backs[1, half, zs] + in_rows[half, zs] + pot_at(half, k) * one) - x
                value = cheb_ref[0] * x + cheb_ref[1] * one + cheb_ref[2] * second
                in_rows[half, zs] = value * value
                return carry

        lax.fori_loop(0, 8, sum_up, 0)

    sum_squares(in_rows, sums, total, qsend, qrecv)

    def density_target(peer):
        rows, cols = tile_at(peer // 2, lax.rem(peer, 2))
        return out_ref.at[:, rows, cols]

    done = Swap(
        QUAD,
        lambda peer: total.at[lax.rem(peer // 4, 2), pl.ds(pl.multiple_of(lax.rem(peer, 4) * 4, 4), 4)],
        density_target,
        dsend,
        drecv,
    )
    done.start()
    to_owner.wait_sends()
    line.wait_sends()
    ring.wait_sends()
    done.wait()


def run(cheb, kb, orbital, pot, packed):
    table = kinetic_table(N)
    high, low = split3(table)
    left = np.concatenate([high, high, low], axis=1)
    side = np.concatenate([table[:128, :128], table[128:, :128]], axis=0)
    high, low = split3(side)
    right = np.concatenate([high, high, low], axis=0)
    off = sphere_offsets()
    marks = np.zeros((136, 128), np.float32)
    rows = np.arange(64)[:, None]
    marks[:64] = rows // 8
    marks[64:128] = off[None, :, 1] + REACH == rows % 8
    marks[128] = off[:, 0]
    marks[129] = off[:, 2]
    kb_row = jnp.pad(kb, (0, 124)).reshape(1, 128)
    field = (2, 128, 8, 128)
    slab = (8, N, 128)
    vmem = pl.BlockSpec(memory_space=pltpu.VMEM)
    anywhere = pl.BlockSpec(memory_space=pl.ANY)
    bf16 = jnp.bfloat16
    return pl.pallas_call(
        program,
        out_shape=jax.ShapeDtypeStruct((4, N, N), F32),
        in_specs=[pl.BlockSpec(memory_space=pltpu.SMEM), vmem] + [anywhere] * 3 + [vmem] * 3,
        out_specs=anywhere,
        scratch_shapes=[
            pltpu.VMEM((16, 4, 16, N), F32),
            pltpu.VMEM(field, F32),
            pltpu.VMEM((2, 16, 8, 16, 128), F32),
            pltpu.VMEM((4, 88, 128), F32),
            pltpu.VMEM((2,) + slab, F32),
            pltpu.VMEM((2,) + field, F32),
            pltpu.VMEM((2,) + field, F32),
            pltpu.VMEM(field, F32),
            pltpu.VMEM(field, F32),
            pltpu.VMEM((2,) + slab, F32),
            pltpu.VMEM((8, 4, 512, 128), F32),
            pltpu.VMEM((8, 512, 128), F32),
            pltpu.VMEM((512, N), F32),
            pltpu.VMEM((512, N), bf16),
            pltpu.VMEM((N, 512), bf16),
            pltpu.VMEM((2, 64, 128), F32),
            pltpu.VMEM((2, 6, 32, 128), F32),
            pltpu.VMEM((64, 128), F32),
            pltpu.VMEM((2, 2, 7, 8, 8, 128), F32),
            pltpu.VMEM((2, 16, 8, 128), F32),
            dma(4), dma(4), dma(16), dma(16), dma(32), dma(32), dma(4), dma(4), dma(2, 8), dma(2, 8),
            dma(2, 32), dma(2, 32), dma(2, 32), dma(2, 32), dma(2), dma(2), dma(2, 6), dma(2, 6),
            dma(2, 2, 7), dma(2, 2, 7), dma(64), dma(64),
        ],
        compiler_params=pltpu.CompilerParams(
            collective_id=1, has_side_effects=True, vmem_limit_bytes=61 * 1024 * 1024
        ),
    )(cheb, kb_row, orbital, pot, packed, left, right, marks)


def local(random_orbitals, potential, sphere_cells, projectors, kb_energy, cheb_coef):
    lanes = lax.broadcasted_iota(jnp.int32, (16, 128), 1)
    centre_z, cell = sphere_cells[:, 0, :1], sphere_cells[:, 1, :1]
    centre_y, centre_x = cell // N, cell % N
    meta = jnp.where(lanes == 0, centre_z, jnp.where(lanes == 1, centre_y, centre_x))
    hit_rows = (centre_y + jnp.arange(8)[None, :] - REACH) % N
    extra = jnp.broadcast_to(hit_rows.reshape(1, 128), (8, 128))
    packed = jnp.concatenate([projectors.reshape(64, SPH), meta.astype(F32), extra.astype(F32)], axis=0)
    return run(cheb_coef, kb_energy, random_orbitals[0], potential, packed)


def solution(mesh):
    apart = Mesh(mesh.devices.reshape([SIZES[name] for name in AXES]), AXES)
    orb, grid = ("y", "xl"), ("xh", "zb", "par", "core")
    in_specs = (P(orb, grid), P(grid), P(grid), P(grid), P(), P())
    return jax.shard_map(local, mesh=apart, in_specs=in_specs, out_specs=P(grid), check_vma=False)
```

```python
import functools

import jax
import jax.numpy as jnp
import numpy as np
from jax import lax
from jax.experimental import pallas as pl
from jax.experimental.pallas import tpu as pltpu
from jax.sharding import Mesh, PartitionSpec as P

AXES = ("y", "xl", "xh", "zb", "par", "core")
SIZES = {"y": 4, "xl": 2, "xh": 2, "zb": 8, "par": 2, "core": 2}
PLANE = ("y", "xl", "xh")
LINE = ("zb", "par", "core")
BLOCK = ("y", "xl", "xh", "par")
QUAD = ("y", "xl", "xh", "par", "core")

N = 256
REACH = 3
SPH = 128
MESH = pl.DeviceIdType.MESH
F32 = jnp.float32


def kinetic_table(length):
    places = np.arange(length)
    offset = places[:, None] - places[None, :]
    parity = np.where(offset % 2 == 0, 1.0, -1.0)
    sine = np.where(offset == 0, 1.0, np.sin(offset * (np.pi / length)))
    table = np.where(offset == 0, length * length / 12.0 + 1.0 / 6.0, parity / (2.0 * sine * sine))
    return (table * (4.0 / (length * length))).astype(np.float32)


def sphere_offsets():
    width = 2 * REACH + 1
    count = width**3
    ids = np.arange(count)
    off = np.stack([ids // (width * width), ids // width % width, ids % width], axis=1) - REACH
    radius = (off * off).sum(axis=1)
    return off[np.argsort(radius * count + ids, kind="stable")[:SPH]]


def index_of(axes):
    where = 0
    for name in axes:
        where = where * SIZES[name] + lax.axis_index(name)
    return where


def coords_of(axes, where):
    coords = {}
    for name in reversed(axes):
        coords[name] = lax.rem(where, SIZES[name])
        where = where // SIZES[name]
    return coords


def group_size(axes):
    return int(np.prod([SIZES[name] for name in axes]))


def greet_group(axes):
    me, count = index_of(axes), group_size(axes)
    barrier = pltpu.get_barrier_semaphore()

    def greet(k, carry):
        pl.semaphore_signal(
            barrier, inc=1, device_id=coords_of(axes, lax.rem(me + k, count)), device_id_type=MESH
        )
        return carry

    lax.fori_loop(1, count, greet, 0)
    return barrier, count - 1


def copy_to(src, dst, send, recv, coords):
    return pltpu.make_async_remote_copy(
        src_ref=src, dst_ref=dst, send_sem=send, recv_sem=recv, device_id=coords, device_id_type=MESH
    )


def dma(*shape):
    return pltpu.SemaphoreType.DMA(shape)


def wait_all(ref, sem):
    pltpu.make_async_copy(ref, ref, sem).wait()


def home_of(block, slab):
    orbital = lax.rem(block + 16 - lax.rem(slab // 2, 16), 8)
    return {
        "y": orbital // 2,
        "xl": lax.rem(orbital, 2),
        "xh": slab // 32,
        "zb": lax.rem(slab // 4, 8),
        "par": lax.rem(slab // 2, 2),
        "core": lax.rem(slab, 2),
    }


def full(coords):
    return tuple(coords[name] for name in AXES)


def is_me(coords):
    same = coords["y"] == lax.axis_index("y")
    for name in AXES[1:]:
        same = jnp.logical_and(same, coords[name] == lax.axis_index(name))
    return same


def pack_atoms(cells_ref, proj_ref, packed):
    packed[0:64, :] = proj_ref[...]
    lanes = lax.broadcasted_iota(jnp.int32, (16, 128), 1)
    centre_z, cell = cells_ref[:, 0, :][:, 0:1], cells_ref[:, 1, :][:, 0:1]
    centre_y, centre_x = cell // N, lax.rem(cell, N)
    meta = jnp.where(lanes == 0, centre_z, jnp.where(lanes == 1, centre_y, centre_x))
    packed[64:80, :] = meta.astype(F32)
    atom = lax.broadcasted_iota(jnp.int32, (16, 128), 0)
    mine = jnp.sum(jnp.where(lanes // 8 == atom, centre_y, 0).astype(F32), axis=0, keepdims=True)
    step = lax.rem(lanes[0:1], 8).astype(F32) - REACH
    packed[80:88, :] = jnp.broadcast_to(wrapped(mine + step), (8, 128))


class Atoms:
    def __init__(self, at_ref, at_out, send, recv):
        slab = index_of(("xh", "zb", "par", "core"))
        there = lax.rem(index_of(("y", "xl")) + index_of(("zb", "par")), 8)
        odd = lax.rem(slab, 2)
        chip, near = slab // 2, lax.rem(slab // 2 + 2 * odd - 1 + 32, 32)
        mine, zb = index_of(BLOCK), lax.axis_index("zb")
        self.refs = (at_ref, at_out, send, recv)
        self.homes = [home_of(zb, lax.rem(2 * mine - 1 + slot + 64, 64)) for slot in range(4)]
        self.sends = []
        for n, (q, slot) in enumerate(((chip, 1 + odd), (near, 3 - 3 * odd))):
            for core in range(2):
                place = coords_of(BLOCK, q)
                place["zb"] = there
                place["core"] = jnp.int32(core)
                self.sends.append((place, slot, 2 * n + core))

    def greet(self, barrier):
        own = jnp.int32(0)
        for home in self.homes:
            same = is_me(home)
            own = own + same.astype(jnp.int32)

            @pl.when(jnp.logical_not(same))
            def _():
                pl.semaphore_signal(barrier, inc=1, device_id=full(home), device_id_type=MESH)

        return 4 - own

    def each(self, go):
        at_ref, at_out, send, recv = self.refs
        for place, slot, n in self.sends:
            same = is_me(place)

            @pl.when(jnp.logical_not(same))
            def _():
                copy = copy_to(at_ref, at_out.at[slot], send.at[n], recv.at[slot], full(place))
                if go:
                    copy.start()
                else:
                    copy.wait_send()

            @pl.when(same)
            def _():
                copy = pltpu.make_async_copy(at_ref, at_out.at[slot], send.at[n])
                if go:
                    copy.start()
                else:
                    copy.wait()

    def start(self):
        self.each(True)

    def wait(self):
        at_ref, at_out, send, recv = self.refs
        self.each(False)
        for slot, home in enumerate(self.homes):
            @pl.when(jnp.logical_not(is_me(home)))
            def _():
                copy_to(at_ref, at_out.at[slot], send.at[0], recv.at[slot], full(home)).wait_recv()


def split3(table):
    high = table.astype(jnp.bfloat16)
    low = (table - high.astype(np.float32)).astype(jnp.bfloat16)
    return high, low


def split(x):
    high = x.astype(jnp.bfloat16)
    return high, (x - high.astype(F32)).astype(jnp.bfloat16)


def mm(a, b):
    return lax.dot_general(a, b, (((1,), (0,)), ((), ())), preferred_element_type=F32)


def mm_nt(a, b):
    return lax.dot_general(a, b, (((1,), (1,)), ((), ())), preferred_element_type=F32)


def wrapped(x):
    x = jnp.where(x < 0.0, x + 256.0, x)
    return jnp.where(x > 255.0, x - 256.0, x)


def along_z(x_ref, out_ref, kl_ref):
    table = kl_ref[...]
    for pair in range(4):
        x = jnp.concatenate(
            [x_ref[:, :, 2 * pair, :].reshape(N, 128), x_ref[:, :, 2 * pair + 1, :].reshape(N, 128)], axis=1
        )
        high, low = split(x)
        res = mm(table, jnp.concatenate([high, low, high], axis=0))
        out_ref[:, :, 2 * pair, :] = res[:, :128].reshape(2, 128, 128)
        out_ref[:, :, 2 * pair + 1, :] = res[:, 128:].reshape(2, 128, 128)


def planes_at(n):
    return n // 4, pl.ds(pl.multiple_of(lax.rem(n, 4) * 32, 32), 32)


def along_x(x_ref, sib_ref, out_ref, kr_ref):
    def step(n, carry):
        half, zs = planes_at(n)
        x = x_ref[half, zs]
        both = jnp.concatenate([x.reshape(256, 128), sib_ref[half, zs].reshape(256, 128)], axis=1)
        high, low = split(both)
        res = mm(jnp.concatenate([high, low, high], axis=1), kr_ref[...])
        out_ref[half, zs] += res.reshape(32, 8, 128) - 2.0 * x
        return carry

    lax.fori_loop(0, 8, step, 0)


def two_planes(z_ref, n):
    return split(jnp.concatenate([z_ref[2 * n], z_ref[2 * n + 1]], axis=1))


def along_y(z_ref, out_ref, kl_ref):
    def step(n, carry):
        high, low = two_planes(z_ref, n)
        res = mm(kl_ref[...], jnp.concatenate([high, low, high], axis=0))
        out_ref[2 * n] = res[:, :128]
        out_ref[2 * n + 1] = res[:, 128:]
        return carry

    lax.fori_loop(0, 4, step, 0)


def build_frames(at_ref, frames, rows_f32, pick, pick_t, marks_ref):
    first_plane = (8 * index_of(BLOCK)).astype(F32)
    first_col = (128 * lax.axis_index("core")).astype(F32)
    dz, dx = marks_ref[128:129, :], marks_ref[129:130, :]

    def step(a, carry):
        slot, i = a // 16, lax.rem(a, 16)
        meta = at_ref[slot, pl.ds(64 + i, 1), :]
        plane = wrapped(meta[:, 0:1] + dz) - first_plane
        col = wrapped(meta[:, 2:3] + dx) - first_col
        mask = jnp.where(plane == marks_ref[0:64, :], marks_ref[64:128, :], 0.0)
        parts = []
        for p in range(4):
            parts.append(mask * at_ref[slot, pl.ds(4 * i + p, 1), :])
        high, low = split(jnp.concatenate(parts, axis=0))
        cols = lax.broadcasted_iota(jnp.int32, (128, 128), 0).astype(F32)
        hit = jnp.where(cols == col, 1.0, 0.0).astype(jnp.bfloat16)
        res = mm_nt(high, hit) + mm_nt(low, hit)
        at = pl.ds(pl.multiple_of(8 * a, 8), 8)
        for p in range(4):
            for z in range(8):
                frames[z, p, at, :] = res[64 * p + 8 * z : 64 * p + 8 * z + 8]
        row = wrapped(meta[:, 1:2] + lax.broadcasted_iota(jnp.int32, (8, 1), 0).astype(F32) - 3.0)
        ys = lax.broadcasted_iota(jnp.int32, (8, N), 1).astype(F32)
        rows_f32[at, :] = jnp.where(ys == row, 1.0, 0.0)
        return carry

    lax.fori_loop(0, 64, step, 0)
    pick[...] = rows_f32[...].astype(jnp.bfloat16)
    ys = lax.broadcasted_iota(jnp.int32, (N, 128), 0).astype(F32)
    for slot in range(4):
        pick_t[:, 128 * slot : 128 * slot + 128] = jnp.where(
            ys == at_ref[slot, 80:81, :], 1.0, 0.0
        ).astype(jnp.bfloat16)


def project(z_ref, picked, frames, pick, part):
    def rows(n, carry):
        high, low = two_planes(z_ref, n)
        res = mm(pick[...], high) + mm(pick[...], low)
        picked[2 * n] = res[:, :128]
        picked[2 * n + 1] = res[:, 128:]
        return carry

    lax.fori_loop(0, 4, rows, 0)
    lanes = lax.broadcasted_iota(jnp.int32, (8, 128), 1)

    def atoms(n, carry):
        at = pl.ds(pl.multiple_of(64 * n, 64), 64)
        sums = [jnp.zeros((64, 128), F32) for _ in range(4)]
        for z in range(8):
            field = picked[z, at, :]
            for p in range(4):
                sums[p] = sums[p] + frames[z, p, at, :] * field
        value = jnp.zeros((8, 128), F32)
        for p in range(4):
            total = jnp.sum(jnp.sum(sums[p].reshape(8, 8, 128), axis=1), axis=1, keepdims=True)
            value = jnp.where(lanes == p, total, value)
        part[pl.ds(pl.multiple_of(8 * n, 8), 8), :] = value
        return carry

    lax.fori_loop(0, 8, atoms, 0)


def spread_back(coeffs, picked, frames, pick_t, out_ref):
    def atoms(n, carry):
        value = coeffs[pl.ds(pl.multiple_of(8 * n, 8), 8), :]
        for i in range(8):
            at = pl.ds(pl.multiple_of(64 * n + 8 * i, 8), 8)
            wide = [jnp.broadcast_to(value[i : i + 1, p : p + 1], (8, 128)) for p in range(4)]
            for z in range(8):
                total = wide[0] * frames[z, 0, at, :]
                for p in range(1, 4):
                    total = total + wide[p] * frames[z, p, at, :]
                picked[z, at, :] = total
        return carry

    lax.fori_loop(0, 8, atoms, 0)

    def planes(n, carry):
        high, low = two_planes(picked, n)
        res = mm(pick_t[...], high) + mm(pick_t[...], low)
        out_ref[2 * n] += res[:, :128]
        out_ref[2 * n + 1] += res[:, 128:]
        return carry

    lax.fori_loop(0, 4, planes, 0)


class Swap:
    def __init__(self, axes, source, target, send, recv, each=False):
        self.axes, self.source, self.target, self.send, self.recv = axes, source, target, send, recv
        self.me, self.each = index_of(axes), each

    def arrived(self, peer):
        return self.recv.at[peer] if self.each else self.recv

    def remote(self, peer):
        return copy_to(
            self.source(peer), self.target(self.me), self.send, self.arrived(self.me), coords_of(self.axes, peer)
        )

    def own(self):
        return pltpu.make_async_copy(self.source(self.me), self.target(self.me), self.arrived(self.me))

    def start(self):
        count = group_size(self.axes)

        def step(k, carry):
            self.remote(lax.rem(self.me + k, count)).start()
            return carry

        lax.fori_loop(1, count, step, 0)
        self.own().start()

    def start_one(self, peer):
        @pl.when(peer != self.me)
        def _():
            self.remote(peer).start()

        @pl.when(peer == self.me)
        def _():
            self.own().start()


def planes_of(field, q):
    return field.at[q // 16, pl.ds(pl.multiple_of(lax.rem(q, 16) * 8, 8), 8)]


def sent_31(field):
    return field.at[:, pl.ds(0, 124)]


def planes_swap(y_ref, z_ref, send, recv):
    return Swap(
        BLOCK,
        lambda peer: planes_of(y_ref, peer),
        lambda peer: z_ref.at[:, pl.ds(pl.multiple_of(peer * 8, 8), 8), :],
        send,
        recv,
    )


def rows_swap(z_ref, y_ref, send, recv):
    return Swap(
        BLOCK,
        lambda peer: z_ref.at[:, pl.ds(pl.multiple_of(peer * 8, 8), 8), :],
        lambda peer: planes_of(y_ref, peer),
        send,
        recv,
    )


def tile_at(rows, cols):
    return pl.ds(pl.multiple_of(rows * 8, 8), 8), pl.ds(pl.multiple_of(cols * 128, 128), 128)


class Ring:
    def __init__(self, ring, send, recv):
        self.refs = (ring, send, recv)
        self.z = index_of(("zb", "par"))
        self.steps = (8, 7)

    def copy(self, way, step):
        ring, send, recv = self.refs
        turn = 1 if way == 0 else 15
        slot = lax.rem(self.z + (16 - step if way == 0 else step), 16)
        return copy_to(
            ring.at[:, slot],
            ring.at[:, slot],
            send,
            recv.at[way, step],
            coords_of(("zb", "par"), lax.rem(self.z + turn, 16)),
        )

    def arrival(self, way, step):
        ring, send, recv = self.refs
        slot = lax.rem(self.z + (15 - step if way == 0 else step + 1), 16)
        turn = 1 if way == 0 else 15
        return copy_to(
            ring.at[:, slot],
            ring.at[:, slot],
            send,
            recv.at[way, step],
            coords_of(("zb", "par"), lax.rem(self.z + turn, 16)),
        )

    def step(self, step):
        for way in range(2):
            if 0 < step <= self.steps[way]:
                self.arrival(way, step - 1).wait_recv()
            if step < self.steps[way]:
                self.copy(way, step).start()

    def wait_sends(self):
        ring, send, _ = self.refs
        wait_all(ring.at[:, pl.ds(0, 15)], send)


class Coeffs:
    def __init__(self, part, got, send, recv):
        core, me = lax.axis_index("core"), index_of(BLOCK)
        up, down = lax.rem(me + 1, 32), lax.rem(me + 31, 32)
        low, high = pl.ds(0, 32), pl.ds(32, 32)

        def place(chip, which):
            coords = coords_of(BLOCK, chip)
            coords["core"] = which
            return coords

        other = {"core": 1 - core}
        self.refs = (got, send, recv)
        self.coords = []
        self.copies = [copy_to(part.at[low], got.at[0], send, recv, other)]
        self.copies.append(copy_to(part.at[high], got.at[1], send, recv, other))
        for n in range(2):
            which = lax.rem(core + n, 2)
            above, below = place(up, which), place(down, which)
            if n == 1:
                self.coords = [above, below]
            self.copies.append(copy_to(part.at[high], got.at[2 + core], send, recv, above))
            self.copies.append(copy_to(part.at[low], got.at[4 + core], send, recv, below))

    def start(self):
        for copy in self.copies:
            copy.start()

    def wait(self):
        got, send, recv = self.refs
        wait_all(got, recv)
        wait_all(got, send)


def sum_squares(squares, sums, total, send, recv):
    zb = lax.axis_index("zb")
    eight = pl.ds(0, 8)

    def flow(way, half, step):
        turn = 1 if way == 0 else 7
        place = {"zb": lax.rem(zb + turn, 8)}
        dst = sums.at[way, half, step]
        return place, dst, send, recv.at[way, half, step]

    def own(way, half, away):
        chunk = lax.rem(zb + (16 - away if way == 0 else away), 8)
        return way, pl.ds(pl.multiple_of(chunk * 16 + half * 8, 8), 8)

    flows = [(way, half) for half in range(2) for way in range(2)]
    for way, half in flows:
        place, dst, one, two = flow(way, half, 0)
        copy_to(squares.at[own(way, half, 1)], dst, one, two, place).start()

    def step(n, carry):
        for way, half in flows:
            place, dst, one, two = flow(way, half, n)
            before, src, was_one, was_two = flow(way, half, n - 1)
            copy_to(src, src, was_one, was_two, before).wait_recv()
            sums[way, half, n - 1] += squares[own(way, half, n + 1)]
            copy_to(src, dst, one, two, place).start()
        return carry

    lax.fori_loop(1, 7, step, 0)
    for way, half in flows:
        place, dst, one, two = flow(way, half, 6)
        copy_to(dst, dst, one, two, place).wait_recv()
        total[way, 8 * half : 8 * half + 8] = (sums[way, half, 6] + squares[own(way, half, 0)]) * 0.125

    wait_all(sums, send)


def program(
    cheb_ref, kb_ref, orbital_ref, pot_ref, cells_ref, proj_ref, kl_ref, kr_ref, marks_ref, out_ref,
    packed, v_rows, v, ring_ref, atoms, planes, sibs, backs, first, in_rows, in_planes, frames, picked, rows_f32,
    pick, pick_t, part, got, coeffs, sums, total, quad,
    asend, arecv, rsend, rrecv, lsend, lrecv, psend, precv, vsend, vrecv,
    zsend, zrecv, ysend, yrecv, ssend, srecv, csend, crecv, qsend, qrecv, dsend, drecv,
):
    core, par, zb, xh = (lax.axis_index(name) for name in ("core", "par", "zb", "xh"))
    plane_me = index_of(PLANE)
    z_me = 2 * zb + par
    shares = [Coeffs(part.at[n], got.at[n], csend.at[n], crecv.at[n]) for n in range(2)]
    barrier, greeted = greet_group(BLOCK)
    greeted = greeted + greet_group(LINE)[1] + 3
    for coords in shares[0].coords + [{"xh": 1 - xh, "core": 1 - core}]:
        pl.semaphore_signal(barrier, inc=1, device_id=coords, device_id_type=MESH)
    spread = Atoms(packed, atoms, asend, arecv)
    greeted = greeted + spread.greet(barrier)
    pack_atoms(cells_ref, proj_ref, packed)
    pl.semaphore_wait(barrier, greeted)

    to_owner = Swap(
        PLANE,
        lambda peer: orbital_ref.at[:, pl.ds(pl.multiple_of(peer * 16, 16), 16), :],
        lambda peer: v_rows.at[peer],
        rsend.at[0],
        rrecv.at[0],
    )
    pot_owner = Swap(
        ("xh", "core"),
        lambda peer: pot_ref.at[
            :,
            pl.ds(pl.multiple_of((plane_me - xh + peer // 2) * 16, 16), 16),
            pl.ds(pl.multiple_of(lax.rem(peer, 2) * 128, 128), 128),
        ],
        lambda peer: ring_ref.at[peer // 2, z_me, pl.ds(pl.multiple_of(lax.rem(peer, 2) * 4, 4), 4)],
        psend.at[0],
        precv.at[0],
    )
    ring = Ring(ring_ref, vsend.at[0], vrecv)
    pot_owner.start()
    to_owner.start()
    spread.start()
    wait_all(ring_ref.at[:, z_me], precv.at[0])
    ring.step(0)
    ring.step(1)

    def line_source(peer):
        rows, cols = tile_at(lax.rem(peer // 2, 2), lax.rem(peer, 2))
        return v_rows.at[pl.ds(peer // 4 * 2, 2), :, rows, cols]

    line = Swap(
        LINE,
        line_source,
        lambda peer: v.at[:, pl.ds(pl.multiple_of(peer * 4, 4), 4)],
        lsend.at[0], lrecv, True,
    )

    def to_block(k, carry):
        there = lax.rem(zb + k, 8)
        for n in range(4):
            line.start_one(4 * there + n)
        return carry

    wait_all(v_rows, rrecv.at[0])
    lax.fori_loop(0, 8, to_block, 0)
    spread.wait()
    build_frames(atoms, frames, rows_f32, pick, pick_t, marks_ref)

    out = planes_swap(v, planes.at[0], zsend.at[0], zrecv.at[0])

    def arrive(k, carry):
        there = lax.rem(zb - k + 8, 8)
        for n in range(4):
            wait_all(line.target(4 * there + n), lrecv.at[4 * there + n])
            if n % 2 == 1:
                z = 2 * there + n // 2
                out.start_one(z)
                out.start_one(16 + z)
        return carry

    lax.fori_loop(0, 8, arrive, 0)
    ring.step(2)

    lanes = lax.broadcasted_iota(jnp.int32, (1, 128), 1)
    energies = jnp.zeros((1, 128), F32)
    for p in range(4):
        energies = jnp.where(lanes == p, kb_ref[p], energies)

    def pot_at(half, n):
        zs = pl.ds(pl.multiple_of(lax.rem(n, 4) * 4, 4), 4)
        rows = pl.ds(pl.multiple_of(par * 8, 8), 8)
        return ring_ref[half, zs, :, rows, :].reshape(32, 8, 128)

    for n in range(2):
        x_ref = v if n == 0 else first
        sib = copy_to(x_ref, sibs.at[n], ssend.at[n], srecv.at[n], {"core": 1 - core})
        if n == 1:
            out = planes_swap(x_ref, planes.at[n], zsend.at[n], zrecv.at[n])
            out.start()
        sib.start()
        along_z(x_ref, in_rows, kl_ref)
        if n == 0:
            ring.step(3)
        sib.wait()
        along_x(x_ref, sibs.at[n], in_rows, kr_ref)
        if n == 0:
            ring.step(4)
        wait_all(planes.at[n], zrecv.at[n])
        share = shares[n]
        project(planes.at[n], picked, frames, pick, part.at[n])
        share.start()
        if n == 0:
            ring.step(5)
        along_y(planes.at[n], in_planes.at[n], kl_ref)
        share.wait()
        if n == 0:
            ring.step(6)
        low, high = pl.ds(0, 32), pl.ds(32, 32)
        own, them = part.at[n], got.at[n]
        coeffs[low, :] = (own[low, :] + them[0] + them[2] + them[3]) * energies
        coeffs[high, :] = (own[high, :] + them[1] + them[4] + them[5]) * energies
        spread_back(coeffs, picked, frames, pick_t, in_planes.at[n])
        back = rows_swap(in_planes.at[n], backs.at[n], ysend.at[n], yrecv.at[n])
        back.start()
        if n == 0:
            ring.step(7)
            ring.step(8)
        wait_all(backs.at[n], yrecv.at[n])

        if n == 0:
            def sum_up(k, carry):
                half, zs = planes_at(k)
                x = v[half, zs]
                first[half, zs] = (backs[0, half, zs] + in_rows[half, zs] + pot_at(half, k) * x) * 0.25
                return carry
        else:
            def sum_up(k, carry):
                half, zs = planes_at(k)
                x, one = v[half, zs], first[half, zs]
                second = 0.5 * (backs[1, half, zs] + in_rows[half, zs] + pot_at(half, k) * one) - x
                value = cheb_ref[0] * x + cheb_ref[1] * one + cheb_ref[2] * second
                in_rows[half, zs] = value * value
                return carry

        lax.fori_loop(0, 8, sum_up, 0)

    sum_squares(in_rows, sums, total, qsend.at[0], qrecv)

    def quad_target(peer):
        rows, cols = tile_at(peer // 2, lax.rem(peer, 2))
        return quad.at[:, :, rows, cols]

    to_core = Swap(
        ("par", "core"),
        lambda peer: total.at[:, pl.ds(pl.multiple_of(peer * 4, 4), 4)],
        quad_target,
        dsend.at[0],
        drecv.at[0],
    )
    to_core.start()
    wait_all(quad, drecv.at[0])
    done = Swap(
        PLANE,
        lambda peer: quad.at[lax.rem(peer, 2)],
        lambda peer: out_ref.at[:, pl.ds(pl.multiple_of(peer * 16, 16), 16), :],
        dsend.at[1],
        drecv.at[1],
    )
    done.start()
    wait_all(v_rows.at[pl.ds(0, 15)], rsend.at[0])
    wait_all(ring_ref.at[0, pl.ds(0, 12), 0], psend.at[0])
    wait_all(sent_31(v), lsend.at[0])
    ring.wait_sends()
    for n in range(2):
        wait_all(sent_31(v), zsend.at[n])
        wait_all(sent_31(v), ysend.at[n])
    wait_all(total.at[:, pl.ds(0, 12)], dsend.at[0])
    wait_all(v_rows.at[pl.ds(0, 15)], dsend.at[1])
    wait_all(out_ref, drecv.at[1])


def run(cheb, kb, orbital, pot, cells, proj):
    table = kinetic_table(N)
    high, low = split3(table)
    left = np.concatenate([high, high, low], axis=1)
    side = np.concatenate([table[:128, :128], table[128:, :128]], axis=0)
    high, low = split3(side)
    right = np.concatenate([high, high, low], axis=0)
    off = sphere_offsets()
    marks = np.zeros((136, 128), np.float32)
    rows = np.arange(64)[:, None]
    marks[:64] = rows // 8
    marks[64:128] = off[None, :, 1] + REACH == rows % 8
    marks[128] = off[:, 0]
    marks[129] = off[:, 2]
    field = (2, 128, 8, 128)
    slab = (8, N, 128)
    vmem = pl.BlockSpec(memory_space=pltpu.VMEM)
    smem = pl.BlockSpec(memory_space=pltpu.SMEM)
    hbm = pl.BlockSpec(memory_space=pltpu.HBM)
    bf16 = jnp.bfloat16
    return pl.pallas_call(
        program,
        out_shape=jax.ShapeDtypeStruct((4, N, N), F32),
        in_specs=[smem] * 2 + [hbm] * 2 + [vmem] * 5,
        out_specs=pl.BlockSpec(memory_space=pl.ANY),
        scratch_shapes=[
            pltpu.VMEM((88, 128), F32),
            pltpu.VMEM((16, 4, 16, N), F32),
            pltpu.VMEM(field, F32),
            pltpu.VMEM((2, 16, 8, 16, 128), F32),
            pltpu.VMEM((4, 88, 128), F32),
            pltpu.VMEM((2,) + slab, F32),
            pltpu.VMEM((2,) + field, F32),
            pltpu.VMEM((2,) + field, F32),
            pltpu.VMEM(field, F32),
            pltpu.VMEM(field, F32),
            pltpu.VMEM((2,) + slab, F32),
            pltpu.VMEM((8, 4, 512, 128), F32),
            pltpu.VMEM((8, 512, 128), F32),
            pltpu.VMEM((512, N), F32),
            pltpu.VMEM((512, N), bf16),
            pltpu.VMEM((N, 512), bf16),
            pltpu.VMEM((2, 64, 128), F32),
            pltpu.VMEM((2, 6, 32, 128), F32),
            pltpu.VMEM((64, 128), F32),
            pltpu.VMEM((2, 2, 7, 8, 8, 128), F32),
            pltpu.VMEM((2, 16, 8, 128), F32),
            pltpu.VMEM((2, 4, 16, N), F32),
            dma(4), dma(4), dma(1), dma(1), dma(1), dma(32), dma(1), dma(1), dma(1), dma(2, 8),
            dma(2), dma(2), dma(2), dma(2), dma(2), dma(2), dma(2), dma(2),
            dma(1), dma(2, 2, 7), dma(2), dma(2),
        ],
        compiler_params=pltpu.CompilerParams(
            collective_id=1, has_side_effects=True, vmem_limit_bytes=62 * 1024 * 1024
        ),
    )(cheb, kb, orbital, pot, cells, proj, left, right, marks)


def local(random_orbitals, potential, sphere_cells, projectors, kb_energy, cheb_coef):
    return run(
        cheb_coef, kb_energy, random_orbitals[0], potential, sphere_cells,
        projectors.reshape(4 * projectors.shape[0], SPH),
    )


def solution(mesh):
    apart = Mesh(mesh.devices.reshape([SIZES[name] for name in AXES]), AXES)
    orb, grid = ("y", "xl"), ("xh", "zb", "par", "core")
    in_specs = (P(orb, grid), P(grid), P(grid), P(grid), P(), P())
    return jax.shard_map(local, mesh=apart, in_specs=in_specs, out_specs=P(grid), check_vma=False)
```

```python
import functools

import jax
import jax.numpy as jnp
import numpy as np
from jax import lax
from jax.experimental import pallas as pl
from jax.experimental.pallas import tpu as pltpu
from jax.sharding import Mesh, PartitionSpec as P

AXES = ("y", "xl", "xh", "zb", "par", "core")
SIZES = {"y": 4, "xl": 2, "xh": 2, "zb": 8, "par": 2, "core": 2}
PLANE = ("y", "xl", "xh")
LINE = ("zb", "par", "core")
BLOCK = ("y", "xl", "xh", "par")
QUAD = ("y", "xl", "xh", "par", "core")

N = 256
REACH = 3
SPH = 128
MESH = pl.DeviceIdType.MESH
F32 = jnp.float32


def kinetic_table(length):
    places = np.arange(length)
    offset = places[:, None] - places[None, :]
    parity = np.where(offset % 2 == 0, 1.0, -1.0)
    sine = np.where(offset == 0, 1.0, np.sin(offset * (np.pi / length)))
    table = np.where(offset == 0, length * length / 12.0 + 1.0 / 6.0, parity / (2.0 * sine * sine))
    return (table * (4.0 / (length * length))).astype(np.float32)


def sphere_offsets():
    width = 2 * REACH + 1
    count = width**3
    ids = np.arange(count)
    off = np.stack([ids // (width * width), ids // width % width, ids % width], axis=1) - REACH
    radius = (off * off).sum(axis=1)
    return off[np.argsort(radius * count + ids, kind="stable")[:SPH]]


def index_of(axes):
    where = 0
    for name in axes:
        where = where * SIZES[name] + lax.axis_index(name)
    return where


def coords_of(axes, where):
    coords = {}
    for name in reversed(axes):
        coords[name] = lax.rem(where, SIZES[name])
        where = where // SIZES[name]
    return coords


def group_size(axes):
    return int(np.prod([SIZES[name] for name in axes]))


def greet_group(axes):
    me, count = index_of(axes), group_size(axes)
    barrier = pltpu.get_barrier_semaphore()

    def greet(k, carry):
        pl.semaphore_signal(
            barrier, inc=1, device_id=coords_of(axes, lax.rem(me + k, count)), device_id_type=MESH
        )
        return carry

    lax.fori_loop(1, count, greet, 0)
    return barrier, count - 1


def copy_to(src, dst, send, recv, coords):
    return pltpu.make_async_remote_copy(
        src_ref=src, dst_ref=dst, send_sem=send, recv_sem=recv, device_id=coords, device_id_type=MESH
    )


def dma(*shape):
    return pltpu.SemaphoreType.DMA(shape)


def wait_all(ref, sem):
    pltpu.make_async_copy(ref, ref, sem).wait()


def home_of(block, slab):
    orbital = lax.rem(block + 16 - lax.rem(slab // 2, 16), 8)
    return {
        "y": orbital // 2,
        "xl": lax.rem(orbital, 2),
        "xh": slab // 32,
        "zb": lax.rem(slab // 4, 8),
        "par": lax.rem(slab // 2, 2),
        "core": lax.rem(slab, 2),
    }


def full(coords):
    return tuple(coords[name] for name in AXES)


def is_me(coords):
    same = coords["y"] == lax.axis_index("y")
    for name in AXES[1:]:
        same = jnp.logical_and(same, coords[name] == lax.axis_index(name))
    return same


def pack_atoms(cells_ref, proj_ref, packed):
    packed[0:64, :] = proj_ref[...]
    lanes = lax.broadcasted_iota(jnp.int32, (16, 128), 1)
    centre_z, cell = cells_ref[:, 0, :][:, 0:1], cells_ref[:, 1, :][:, 0:1]
    centre_y, centre_x = cell // N, lax.rem(cell, N)
    meta = jnp.where(lanes == 0, centre_z, jnp.where(lanes == 1, centre_y, centre_x))
    packed[64:80, :] = meta.astype(F32)
    atom = lax.broadcasted_iota(jnp.int32, (16, 128), 0)
    mine = jnp.sum(jnp.where(lanes // 8 == atom, centre_y, 0).astype(F32), axis=0, keepdims=True)
    step = lax.rem(lanes[0:1], 8).astype(F32) - REACH
    packed[80:88, :] = jnp.broadcast_to(wrapped(mine + step), (8, 128))


class Atoms:
    def __init__(self, at_ref, at_out, send, recv):
        slab = index_of(("xh", "zb", "par", "core"))
        there = lax.rem(index_of(("y", "xl")) + index_of(("zb", "par")), 8)
        odd = lax.rem(slab, 2)
        chip, near = slab // 2, lax.rem(slab // 2 + 2 * odd - 1 + 32, 32)
        mine, zb = index_of(BLOCK), lax.axis_index("zb")
        self.refs = (at_ref, at_out, send, recv)
        self.homes = [home_of(zb, lax.rem(2 * mine - 1 + slot + 64, 64)) for slot in range(4)]
        self.sends = []
        for n, (q, slot) in enumerate(((chip, 1 + odd), (near, 3 - 3 * odd))):
            for core in range(2):
                place = coords_of(BLOCK, q)
                place["zb"] = there
                place["core"] = jnp.int32(core)
                self.sends.append((place, slot, 2 * n + core))

    def greet(self, barrier):
        own = jnp.int32(0)
        for home in self.homes:
            same = is_me(home)
            own = own + same.astype(jnp.int32)

            @pl.when(jnp.logical_not(same))
            def _():
                pl.semaphore_signal(barrier, inc=1, device_id=full(home), device_id_type=MESH)

        return 4 - own

    def each(self, go):
        at_ref, at_out, send, recv = self.refs
        for place, slot, n in self.sends:
            same = is_me(place)

            @pl.when(jnp.logical_not(same))
            def _():
                copy = copy_to(at_ref, at_out.at[slot], send.at[n], recv.at[slot], full(place))
                if go:
                    copy.start()
                else:
                    copy.wait_send()

            @pl.when(same)
            def _():
                copy = pltpu.make_async_copy(at_ref, at_out.at[slot], send.at[n])
                if go:
                    copy.start()
                else:
                    copy.wait()

    def start(self):
        self.each(True)

    def wait(self):
        at_ref, at_out, send, recv = self.refs
        self.each(False)
        for slot, home in enumerate(self.homes):
            @pl.when(jnp.logical_not(is_me(home)))
            def _():
                copy_to(at_ref, at_out.at[slot], send.at[0], recv.at[slot], full(home)).wait_recv()


def split3(table):
    high = table.astype(jnp.bfloat16)
    low = (table - high.astype(np.float32)).astype(jnp.bfloat16)
    return high, low


def split(x):
    high = x.astype(jnp.bfloat16)
    return high, (x - high.astype(F32)).astype(jnp.bfloat16)


def mm(a, b):
    return lax.dot_general(a, b, (((1,), (0,)), ((), ())), preferred_element_type=F32)


def mm_nt(a, b):
    return lax.dot_general(a, b, (((1,), (1,)), ((), ())), preferred_element_type=F32)


def wrapped(x):
    x = jnp.where(x < 0.0, x + 256.0, x)
    return jnp.where(x > 255.0, x - 256.0, x)


def along_z(x_ref, out_ref, kl_ref):
    table = kl_ref[...]
    for pair in range(4):
        x = jnp.concatenate(
            [x_ref[:, :, 2 * pair, :].reshape(N, 128), x_ref[:, :, 2 * pair + 1, :].reshape(N, 128)], axis=1
        )
        high, low = split(x)
        res = mm(table, jnp.concatenate([high, low, high], axis=0))
        out_ref[:, :, 2 * pair, :] = res[:, :128].reshape(2, 128, 128)
        out_ref[:, :, 2 * pair + 1, :] = res[:, 128:].reshape(2, 128, 128)


def planes_at(n):
    return n // 4, pl.ds(pl.multiple_of(lax.rem(n, 4) * 32, 32), 32)


def along_x(x_ref, sib_ref, out_ref, kr_ref):
    def step(n, carry):
        half, zs = planes_at(n)
        x = x_ref[half, zs]
        both = jnp.concatenate([x.reshape(256, 128), sib_ref[half, zs].reshape(256, 128)], axis=1)
        high, low = split(both)
        res = mm(jnp.concatenate([high, low, high], axis=1), kr_ref[...])
        out_ref[half, zs] += res.reshape(32, 8, 128) - 2.0 * x
        return carry

    lax.fori_loop(0, 8, step, 0)


REACHED = (range(0, 3), range(0, 7), range(1, 8), range(5, 8))


def two_planes(z_ref, n):
    return split(jnp.concatenate([z_ref[2 * n], z_ref[2 * n + 1]], axis=1))


def along_y(z_ref, out_ref, kl_ref):
    def step(n, carry):
        high, low = two_planes(z_ref, n)
        res = mm(kl_ref[...], jnp.concatenate([high, low, high], axis=0))
        out_ref[2 * n] = res[:, :128]
        out_ref[2 * n + 1] = res[:, 128:]
        return carry

    lax.fori_loop(0, 4, step, 0)


def build_frames(at_ref, frames, rows_f32, pick, pick_t, marks_ref):
    first_plane = (8 * index_of(BLOCK)).astype(F32)
    first_col = (128 * lax.axis_index("core")).astype(F32)
    dz, dx = marks_ref[128:129, :], marks_ref[129:130, :]

    def step(a, carry):
        slot, i = a // 16, lax.rem(a, 16)
        meta = at_ref[slot, pl.ds(64 + i, 1), :]
        plane = wrapped(meta[:, 0:1] + dz) - first_plane
        col = wrapped(meta[:, 2:3] + dx) - first_col
        mask = jnp.where(plane == marks_ref[0:64, :], marks_ref[64:128, :], 0.0)
        parts = []
        for p in range(4):
            parts.append(mask * at_ref[slot, pl.ds(4 * i + p, 1), :])
        high, low = split(jnp.concatenate(parts, axis=0))
        cols = lax.broadcasted_iota(jnp.int32, (128, 128), 0).astype(F32)
        hit = jnp.where(cols == col, 1.0, 0.0).astype(jnp.bfloat16)
        res = mm_nt(high, hit) + mm_nt(low, hit)
        at = pl.ds(pl.multiple_of(8 * a, 8), 8)
        for p in range(4):
            for z in range(8):
                frames[z, p, at, :] = res[64 * p + 8 * z : 64 * p + 8 * z + 8]
        row = wrapped(meta[:, 1:2] + lax.broadcasted_iota(jnp.int32, (8, 1), 0).astype(F32) - 3.0)
        ys = lax.broadcasted_iota(jnp.int32, (8, N), 1).astype(F32)
        rows_f32[at, :] = jnp.where(ys == row, 1.0, 0.0)
        return carry

    lax.fori_loop(0, 64, step, 0)
    pick[...] = rows_f32[...].astype(jnp.bfloat16)
    ys = lax.broadcasted_iota(jnp.int32, (N, 128), 0).astype(F32)
    for slot in range(4):
        pick_t[:, 128 * slot : 128 * slot + 128] = jnp.where(
            ys == at_ref[slot, 80:81, :], 1.0, 0.0
        ).astype(jnp.bfloat16)


def project(z_ref, picked, frames, pick, part):
    def rows(n, carry):
        high, low = two_planes(z_ref, n)
        res = mm(pick[...], high) + mm(pick[...], low)
        picked[2 * n] = res[:, :128]
        picked[2 * n + 1] = res[:, 128:]
        return carry

    lax.fori_loop(0, 4, rows, 0)
    lanes = lax.broadcasted_iota(jnp.int32, (8, 128), 1)

    def atoms(planes, n, carry):
        at = pl.ds(pl.multiple_of(64 * n, 64), 64)
        sums = [jnp.zeros((64, 128), F32) for _ in range(4)]
        for z in planes:
            field = picked[z, at, :]
            for p in range(4):
                sums[p] = sums[p] + frames[z, p, at, :] * field
        value = jnp.zeros((8, 128), F32)
        for p in range(4):
            total = jnp.sum(jnp.sum(sums[p].reshape(8, 8, 128), axis=1), axis=1, keepdims=True)
            value = jnp.where(lanes == p, total, value)
        part[pl.ds(pl.multiple_of(8 * n, 8), 8), :] = value
        return carry

    for slot, planes in enumerate(REACHED):
        lax.fori_loop(2 * slot, 2 * slot + 2, functools.partial(atoms, planes), 0)


def spread_back(coeffs, picked, frames, pick_t, out_ref):
    def atoms(planes, n, carry):
        value = coeffs[pl.ds(pl.multiple_of(8 * n, 8), 8), :]
        for i in range(8):
            at = pl.ds(pl.multiple_of(64 * n + 8 * i, 8), 8)
            wide = [jnp.broadcast_to(value[i : i + 1, p : p + 1], (8, 128)) for p in range(4)]
            for z in range(8):
                if z not in planes:
                    picked[z, at, :] = jnp.zeros((8, 128), F32)
                    continue
                total = wide[0] * frames[z, 0, at, :]
                for p in range(1, 4):
                    total = total + wide[p] * frames[z, p, at, :]
                picked[z, at, :] = total
        return carry

    for slot, planes in enumerate(REACHED):
        lax.fori_loop(2 * slot, 2 * slot + 2, functools.partial(atoms, planes), 0)

    def rows(n, carry):
        high, low = two_planes(picked, n)
        res = mm(pick_t[...], high) + mm(pick_t[...], low)
        out_ref[2 * n] += res[:, :128]
        out_ref[2 * n + 1] += res[:, 128:]
        return carry

    lax.fori_loop(0, 4, rows, 0)


def zigzag(k, count):
    odd = lax.rem(k, 2)
    return lax.rem(count + (2 * odd - 1) * ((k + 1) // 2), count)


class Swap:
    def __init__(self, axes, source, target, send, recv, each=False):
        self.axes, self.source, self.target, self.send, self.recv = axes, source, target, send, recv
        self.me, self.each = index_of(axes), each

    def arrived(self, peer):
        return self.recv.at[peer] if self.each else self.recv

    def remote(self, peer):
        return copy_to(
            self.source(peer), self.target(self.me), self.send, self.arrived(self.me), coords_of(self.axes, peer)
        )

    def own(self):
        return pltpu.make_async_copy(self.source(self.me), self.target(self.me), self.arrived(self.me))

    def start(self):
        count = group_size(self.axes)

        def step(k, carry):
            self.remote(lax.rem(self.me + zigzag(k, count), count)).start()
            return carry

        lax.fori_loop(1, count, step, 0)
        self.own().start()

    def start_one(self, peer):
        @pl.when(peer != self.me)
        def _():
            self.remote(peer).start()

        @pl.when(peer == self.me)
        def _():
            self.own().start()


def planes_of(field, q):
    return field.at[q // 16, pl.ds(pl.multiple_of(lax.rem(q, 16) * 8, 8), 8)]


def sent_31(field):
    return field.at[:, pl.ds(0, 124)]


def planes_swap(y_ref, z_ref, send, recv):
    return Swap(
        BLOCK,
        lambda peer: planes_of(y_ref, peer),
        lambda peer: z_ref.at[:, pl.ds(pl.multiple_of(peer * 8, 8), 8), :],
        send,
        recv,
    )


def rows_swap(z_ref, y_ref, send, recv):
    return Swap(
        BLOCK,
        lambda peer: z_ref.at[:, pl.ds(pl.multiple_of(peer * 8, 8), 8), :],
        lambda peer: planes_of(y_ref, peer),
        send,
        recv,
    )


def tile_at(rows, cols):
    return pl.ds(pl.multiple_of(rows * 8, 8), 8), pl.ds(pl.multiple_of(cols * 128, 128), 128)


class Ring:
    def __init__(self, ring, send, recv):
        self.refs = (ring, send, recv)
        self.z = index_of(("zb", "par"))
        self.steps = (8, 7)

    def copy(self, way, step):
        ring, send, recv = self.refs
        turn = 1 if way == 0 else 15
        slot = lax.rem(self.z + (16 - step if way == 0 else step), 16)
        return copy_to(
            ring.at[:, slot],
            ring.at[:, slot],
            send,
            recv.at[way, step],
            coords_of(("zb", "par"), lax.rem(self.z + turn, 16)),
        )

    def arrival(self, way, step):
        ring, send, recv = self.refs
        slot = lax.rem(self.z + (15 - step if way == 0 else step + 1), 16)
        turn = 1 if way == 0 else 15
        return copy_to(
            ring.at[:, slot],
            ring.at[:, slot],
            send,
            recv.at[way, step],
            coords_of(("zb", "par"), lax.rem(self.z + turn, 16)),
        )

    def step(self, step):
        for way in range(2):
            if 0 < step <= self.steps[way]:
                self.arrival(way, step - 1).wait_recv()
            if step < self.steps[way]:
                self.copy(way, step).start()

    def wait_sends(self):
        ring, send, _ = self.refs
        wait_all(ring.at[:, pl.ds(0, 15)], send)


class Coeffs:
    def __init__(self, part, got, send, recv):
        core, me = lax.axis_index("core"), index_of(BLOCK)
        up, down = lax.rem(me + 1, 32), lax.rem(me + 31, 32)
        low, high = pl.ds(0, 32), pl.ds(32, 32)

        def place(chip, which):
            coords = coords_of(BLOCK, chip)
            coords["core"] = which
            return coords

        other = {"core": 1 - core}
        self.refs = (got, send, recv)
        self.coords = []
        self.copies = [copy_to(part.at[low], got.at[0], send, recv, other)]
        self.copies.append(copy_to(part.at[high], got.at[1], send, recv, other))
        for n in range(2):
            which = lax.rem(core + n, 2)
            above, below = place(up, which), place(down, which)
            if n == 1:
                self.coords = [above, below]
            self.copies.append(copy_to(part.at[high], got.at[2 + core], send, recv, above))
            self.copies.append(copy_to(part.at[low], got.at[4 + core], send, recv, below))

    def start(self):
        for copy in self.copies:
            copy.start()

    def wait(self):
        got, send, recv = self.refs
        wait_all(got, recv)
        wait_all(got, send)


def sum_squares(squares, sums, total, send, recv):
    zb = lax.axis_index("zb")

    def flow(way, half, step):
        turn = 1 if way == 0 else 7
        place = {"zb": lax.rem(zb + turn, 8)}
        dst = sums.at[way, half, step]
        return place, dst, send, recv.at[way, half, step]

    def own(way, half, away):
        chunk = lax.rem(zb + (16 - away if way == 0 else away), 8)
        return way, pl.ds(pl.multiple_of(chunk * 16 + half * 4, 4), 4)

    flows = [(way, half) for half in range(4) for way in range(2)]
    for way, half in flows:
        place, dst, one, two = flow(way, half, 0)
        copy_to(squares.at[own(way, half, 1)], dst, one, two, place).start()

    def step(n, carry):
        for way, half in flows:
            place, dst, one, two = flow(way, half, n)
            before, src, was_one, was_two = flow(way, half, n - 1)
            copy_to(src, src, was_one, was_two, before).wait_recv()
            sums[way, half, n - 1] += squares[own(way, half, n + 1)]
            copy_to(src, dst, one, two, place).start()
        return carry

    lax.fori_loop(1, 7, step, 0)
    for way, half in flows:
        place, dst, one, two = flow(way, half, 6)
        copy_to(dst, dst, one, two, place).wait_recv()
        total[way, 4 * half : 4 * half + 4] = (sums[way, half, 6] + squares[own(way, half, 0)]) * 0.125

    wait_all(sums, send)


def program(
    cheb_ref, kb_ref, orbital_ref, pot_ref, cells_ref, proj_ref, kl_ref, kr_ref, marks_ref, out_ref,
    packed, v_rows, v, ring_ref, atoms, planes, sibs, backs, first, in_rows, in_planes, frames, picked, rows_f32,
    pick, pick_t, part, got, coeffs, sums, total, quad,
    asend, arecv, rsend, rrecv, lsend, lrecv, psend, precv, vsend, vrecv,
    zsend, zrecv, ysend, yrecv, ssend, srecv, csend, crecv, qsend, qrecv, dsend, drecv,
):
    core, par, zb, xh = (lax.axis_index(name) for name in ("core", "par", "zb", "xh"))
    plane_me = index_of(PLANE)
    z_me = 2 * zb + par
    shares = [Coeffs(part.at[n], got.at[n], csend.at[n], crecv.at[n]) for n in range(2)]
    barrier, greeted = greet_group(BLOCK)
    greeted = greeted + greet_group(LINE)[1] + 3
    for coords in shares[0].coords + [{"xh": 1 - xh, "core": 1 - core}]:
        pl.semaphore_signal(barrier, inc=1, device_id=coords, device_id_type=MESH)
    spread = Atoms(packed, atoms, asend, arecv)
    greeted = greeted + spread.greet(barrier)
    pack_atoms(cells_ref, proj_ref, packed)
    pl.semaphore_wait(barrier, greeted)

    to_owner = Swap(
        PLANE,
        lambda peer: orbital_ref.at[:, pl.ds(pl.multiple_of(peer * 16, 16), 16), :],
        lambda peer: v_rows.at[peer],
        rsend.at[0],
        rrecv.at[0],
    )
    pot_owner = Swap(
        ("xh", "core"),
        lambda peer: pot_ref.at[
            :,
            pl.ds(pl.multiple_of((plane_me - xh + peer // 2) * 16, 16), 16),
            pl.ds(pl.multiple_of(lax.rem(peer, 2) * 128, 128), 128),
        ],
        lambda peer: ring_ref.at[peer // 2, z_me, pl.ds(pl.multiple_of(lax.rem(peer, 2) * 4, 4), 4)],
        psend.at[0],
        precv.at[0],
    )
    ring = Ring(ring_ref, vsend.at[0], vrecv)
    pot_owner.start()
    to_owner.start()
    spread.start()
    wait_all(ring_ref.at[:, z_me], precv.at[0])
    ring.step(0)
    ring.step(1)

    def line_source(peer):
        rows, cols = tile_at(lax.rem(peer // 2, 2), lax.rem(peer, 2))
        return v_rows.at[pl.ds(peer // 4 * 2, 2), :, rows, cols]

    line = Swap(
        LINE,
        line_source,
        lambda peer: v.at[:, pl.ds(pl.multiple_of(peer * 4, 4), 4)],
        lsend.at[0], lrecv, True,
    )

    def to_block(k, carry):
        there = lax.rem(zb + zigzag(k, 8), 8)
        for n in range(4):
            line.start_one(4 * there + n)
        return carry

    wait_all(v_rows, rrecv.at[0])
    lax.fori_loop(0, 8, to_block, 0)
    spread.wait()
    build_frames(atoms, frames, rows_f32, pick, pick_t, marks_ref)

    out = planes_swap(v, planes.at[0], zsend.at[0], zrecv.at[0])

    def arrive(k, carry):
        there = lax.rem(zb + 8 - zigzag(k, 8), 8)
        for n in range(4):
            wait_all(line.target(4 * there + n), lrecv.at[4 * there + n])
            if n % 2 == 1:
                z = 2 * there + n // 2
                out.start_one(z)
                out.start_one(16 + z)
        return carry

    lax.fori_loop(0, 8, arrive, 0)
    ring.step(2)

    lanes = lax.broadcasted_iota(jnp.int32, (1, 128), 1)
    energies = jnp.zeros((1, 128), F32)
    for p in range(4):
        energies = jnp.where(lanes == p, kb_ref[p], energies)

    def pot_at(half, n):
        zs = pl.ds(pl.multiple_of(lax.rem(n, 4) * 4, 4), 4)
        rows = pl.ds(pl.multiple_of(par * 8, 8), 8)
        return ring_ref[half, zs, :, rows, :].reshape(32, 8, 128)

    for n in range(2):
        x_ref = v if n == 0 else first
        sib = copy_to(x_ref, sibs.at[n], ssend.at[n], srecv.at[n], {"core": 1 - core})
        if n == 1:
            out = planes_swap(x_ref, planes.at[n], zsend.at[n], zrecv.at[n])
            out.start()
        sib.start()
        along_z(x_ref, in_rows, kl_ref)
        if n == 0:
            ring.step(3)
        sib.wait()
        along_x(x_ref, sibs.at[n], in_rows, kr_ref)
        if n == 0:
            ring.step(4)
        wait_all(planes.at[n], zrecv.at[n])
        share = shares[n]
        project(planes.at[n], picked, frames, pick, part.at[n])
        share.start()
        if n == 0:
            ring.step(5)
        along_y(planes.at[n], in_planes.at[n], kl_ref)
        share.wait()
        if n == 0:
            ring.step(6)
        low, high = pl.ds(0, 32), pl.ds(32, 32)
        own, them = part.at[n], got.at[n]
        coeffs[low, :] = (own[low, :] + them[0] + them[2] + them[3]) * energies
        coeffs[high, :] = (own[high, :] + them[1] + them[4] + them[5]) * energies
        spread_back(coeffs, picked, frames, pick_t, in_planes.at[n])
        back = rows_swap(in_planes.at[n], backs.at[n], ysend.at[n], yrecv.at[n])
        back.start()
        if n == 0:
            ring.step(7)
            ring.step(8)
        wait_all(backs.at[n], yrecv.at[n])

        if n == 0:
            def sum_up(k, carry):
                half, zs = planes_at(k)
                x = v[half, zs]
                first[half, zs] = (backs[0, half, zs] + in_rows[half, zs] + pot_at(half, k) * x) * 0.25
                return carry
        else:
            def sum_up(k, carry):
                half, zs = planes_at(k)
                x, one = v[half, zs], first[half, zs]
                second = 0.5 * (backs[1, half, zs] + in_rows[half, zs] + pot_at(half, k) * one) - x
                value = cheb_ref[0] * x + cheb_ref[1] * one + cheb_ref[2] * second
                in_rows[half, zs] = value * value
                return carry

        lax.fori_loop(0, 8, sum_up, 0)

    sum_squares(in_rows, sums, total, qsend.at[0], qrecv)

    def quad_target(peer):
        rows, cols = tile_at(peer // 2, lax.rem(peer, 2))
        return quad.at[:, :, rows, cols]

    to_core = Swap(
        ("par", "core"),
        lambda peer: total.at[:, pl.ds(pl.multiple_of(peer * 4, 4), 4)],
        quad_target,
        dsend.at[0],
        drecv.at[0],
    )
    to_core.start()
    wait_all(quad, drecv.at[0])
    done = Swap(
        PLANE,
        lambda peer: quad.at[lax.rem(peer, 2)],
        lambda peer: out_ref.at[:, pl.ds(pl.multiple_of(peer * 16, 16), 16), :],
        dsend.at[1],
        drecv.at[1],
    )
    done.start()
    wait_all(v_rows.at[pl.ds(0, 15)], rsend.at[0])
    wait_all(ring_ref.at[0, pl.ds(0, 12), 0], psend.at[0])
    wait_all(sent_31(v), lsend.at[0])
    ring.wait_sends()
    for n in range(2):
        wait_all(sent_31(v), zsend.at[n])
        wait_all(sent_31(v), ysend.at[n])
    wait_all(total.at[:, pl.ds(0, 12)], dsend.at[0])
    wait_all(v_rows.at[pl.ds(0, 15)], dsend.at[1])
    wait_all(out_ref, drecv.at[1])


def run(cheb, kb, orbital, pot, cells, proj):
    table = kinetic_table(N)
    high, low = split3(table)
    left = np.concatenate([high, high, low], axis=1)
    side = np.concatenate([table[:128, :128], table[128:, :128]], axis=0)
    high, low = split3(side)
    right = np.concatenate([high, high, low], axis=0)
    off = sphere_offsets()
    marks = np.zeros((136, 128), np.float32)
    rows = np.arange(64)[:, None]
    marks[:64] = rows // 8
    marks[64:128] = off[None, :, 1] + REACH == rows % 8
    marks[128] = off[:, 0]
    marks[129] = off[:, 2]
    field = (2, 128, 8, 128)
    slab = (8, N, 128)
    vmem = pl.BlockSpec(memory_space=pltpu.VMEM)
    smem = pl.BlockSpec(memory_space=pltpu.SMEM)
    hbm = pl.BlockSpec(memory_space=pltpu.HBM)
    bf16 = jnp.bfloat16
    return pl.pallas_call(
        program,
        out_shape=jax.ShapeDtypeStruct((4, N, N), F32),
        in_specs=[smem] * 2 + [hbm] * 2 + [vmem] * 5,
        out_specs=pl.BlockSpec(memory_space=pl.ANY),
        scratch_shapes=[
            pltpu.VMEM((88, 128), F32),
            pltpu.VMEM((16, 4, 16, N), F32),
            pltpu.VMEM(field, F32),
            pltpu.VMEM((2, 16, 8, 16, 128), F32),
            pltpu.VMEM((4, 88, 128), F32),
            pltpu.VMEM((2,) + slab, F32),
            pltpu.VMEM((2,) + field, F32),
            pltpu.VMEM((2,) + field, F32),
            pltpu.VMEM(field, F32),
            pltpu.VMEM(field, F32),
            pltpu.VMEM((2,) + slab, F32),
            pltpu.VMEM((8, 4, 512, 128), F32),
            pltpu.VMEM((8, 512, 128), F32),
            pltpu.VMEM((512, N), F32),
            pltpu.VMEM((512, N), bf16),
            pltpu.VMEM((N, 512), bf16),
            pltpu.VMEM((2, 64, 128), F32),
            pltpu.VMEM((2, 6, 32, 128), F32),
            pltpu.VMEM((64, 128), F32),
            pltpu.VMEM((2, 4, 7, 4, 8, 128), F32),
            pltpu.VMEM((2, 16, 8, 128), F32),
            pltpu.VMEM((2, 4, 16, N), F32),
            dma(4), dma(4), dma(1), dma(1), dma(1), dma(32), dma(1), dma(1), dma(1), dma(2, 8),
            dma(2), dma(2), dma(2), dma(2), dma(2), dma(2), dma(2), dma(2),
            dma(1), dma(2, 4, 7), dma(2), dma(2),
        ],
        compiler_params=pltpu.CompilerParams(
            collective_id=1, has_side_effects=True, vmem_limit_bytes=62 * 1024 * 1024
        ),
    )(cheb, kb, orbital, pot, cells, proj, left, right, marks)


def local(random_orbitals, potential, sphere_cells, projectors, kb_energy, cheb_coef):
    return run(
        cheb_coef, kb_energy, random_orbitals[0], potential, sphere_cells,
        projectors.reshape(4 * projectors.shape[0], SPH),
    )


def solution(mesh):
    apart = Mesh(mesh.devices.reshape([SIZES[name] for name in AXES]), AXES)
    orb, grid = ("y", "xl"), ("xh", "zb", "par", "core")
    in_specs = (P(orb, grid), P(grid), P(grid), P(grid), P(), P())
    return jax.shard_map(local, mesh=apart, in_specs=in_specs, out_specs=P(grid), check_vma=False)
```
